128 devices in a mesh: wide: 32 (over x, y, core), narrow: 4 (over z).
Axes of the slice: x: 4, y: 4, z: 4, core: 2. Of those that a mesh axis runs over, the one named last changes fastest.
Arguments:
- features: bfloat16 [512, 32, 32, 8, 128], P('wide', None, 'narrow'), may hold values from -6 to 6
- occupied: int32 [512], P('wide'), may hold values from 0 to 1, as said below
- w_first: bfloat16 [32, 32, 3, 3, 3], replicated, may hold values from -0.21875 to 0.21875
- w_second: bfloat16 [32, 32, 3, 3, 3], replicated, may hold values from -0.21875 to 0.21875
- w_head: bfloat16 [3, 32], replicated, may hold values from -1 to 1
Outputs:
- affinities: bfloat16 [512, 3, 32, 8, 128], P('wide', None, 'narrow')
The draws below stay inside these ranges and needn't reach their ends.
Inputs may be any that keep to these rules, and one draw needn't show every extreme that they name: Some index of wide has all 16 of its blocks occupied; in all, between (5) * 32 + 2 and 192 blocks are occupied.
All inputs are finite; a program needn't handle non-finite values.
Results may differ from the reference program's by a relative error of at most 0.0051.
Values may be sent and summed in bfloat16 or wider, within the bound.
A program may use at most 128 MiB of HBM per device.

```python
import jax
import jax.numpy as jnp
from jax import lax

C = 32
AFF = 3
BX = 128
BY = 8
ZD = 8
MARGIN = 2
BLK = 16
CAP = 6
TZ = 12
BLOCKS = 512
NZ = 32
N_WIDE = 32


def draw_occupied(key, part):
    key = jax.random.fold_in(key, 11)
    subkeys = jax.random.split(key, 4)
    shortfall = jax.random.randint(subkeys[0], (), 0, N_WIDE - 1)
    overall = CAP * N_WIDE - shortfall
    busiest = jax.random.randint(subkeys[1], (), 0, N_WIDE)
    places = jnp.arange(N_WIDE)
    weights = jax.random.randint(subkeys[2], (N_WIDE,), 1, 3)
    weights = jnp.where(places == busiest, 0, weights)
    remaining = overall - BLK
    shares = remaining * weights // jnp.sum(weights)
    leftover = remaining - jnp.sum(shares)
    ranked = jnp.cumsum((weights > 0).astype(jnp.int32))
    additions = ((weights > 0) & (ranked <= leftover)).astype(jnp.int32)
    counts = jnp.where(places == busiest, BLK, shares + additions)

    def shuffled(subkey):
        return jax.random.permutation(subkey, BLK)
    orders = jax.vmap(shuffled)(jax.random.split(subkeys[3], N_WIDE))
    return (orders < counts[:, None]).astype(jnp.int32).reshape(N_WIDE * BLK)


def block_levels(key, shape, shards, smallest, top_value):
    gain = 1.0
    for position, parts in shards:
        draws = jax.random.uniform(jax.random.fold_in(jax.random.fold_in(key, 6), position), (parts,), jnp.float32, smallest / len(shards), top_value / len(shards))
        gain = gain * jnp.repeat(jnp.exp(draws), shape[position] // parts).reshape((-1,) + (1,) * (len(shape) - 1 - position))
    return gain


def centred(key, shape, spread, reach, cuts=(), held_as=jnp.bfloat16):
    drawn = jax.random.normal(key, shape, jnp.float32) * spread
    if len(cuts) > 0:
        drawn = block_levels(key, shape, cuts, -0.22, 0.18) * drawn
    return jnp.clip(drawn, min=-reach, max=reach).astype(held_as)


def setup_inputs(seed: int = 0) -> dict:
    seeds = jax.random.split(jax.random.key(seed), 6)
    features = centred(seeds[0], (BLOCKS, C, NZ, BY, BX), 1.0, 6.0, ((0, 32), (2, 4)))
    occupied = draw_occupied(jax.random.fold_in(seeds[5], 71), 0)
    w_first = centred(seeds[2], (C, C, 3, 3, 3), (27 * C) ** -0.5, 0.21875)
    w_second = centred(seeds[3], (C, C, 3, 3, 3), (27 * C) ** -0.5, 0.21875)
    w_head = centred(seeds[4], (AFF, C), C ** -0.5, 1.0)
    return dict(features=features, occupied=occupied, w_first=w_first, w_second=w_second, w_head=w_head)


def blend_table(tile_depth):
    places = jnp.arange(tile_depth).astype(jnp.float32)
    rising = (places + 0.5) / (2 * MARGIN)
    falling = (tile_depth - places - 0.5) / (2 * MARGIN)
    return jnp.minimum(1.0, jnp.minimum(rising, falling))


def convolve(inputs, kernel):
    return lax.conv_general_dilated(inputs, kernel, (1, 1, 1), "SAME", dimension_numbers=("NCDHW", "OIDHW", "NCDHW"), precision=lax.Precision.HIGHEST, preferred_element_type=jnp.float32)


def network(stacked, first_kernel, second_kernel, head_kernel):
    first_act = jax.nn.relu(convolve(stacked, first_kernel)).astype(jnp.bfloat16)
    first_act = lax.optimization_barrier(first_act).astype(jnp.float32)
    second_act = jax.nn.relu(convolve(first_act, second_kernel) + stacked).astype(jnp.bfloat16)
    second_act = lax.optimization_barrier(second_act).astype(jnp.float32)
    logits = jnp.einsum("ac,nczyx->nazyx", head_kernel, second_act, precision=lax.Precision.HIGHEST)
    return logits * blend_table(TZ)[None, None, :, None, None]


def reference(features, occupied, w_first, w_second, w_head):
    first_kernel = w_first.astype(jnp.float32)
    second_kernel = w_second.astype(jnp.float32)
    head_kernel = w_head.astype(jnp.float32)
    blending = blend_table(TZ)
    full_depth = NZ + 2 * MARGIN
    tile_total = NZ // ZD
    coverage = jnp.zeros((full_depth,), jnp.float32)
    for tile_index in range(tile_total):
        coverage = coverage.at[tile_index * ZD:tile_index * ZD + TZ].add(blending)
    coverage = coverage[MARGIN:MARGIN + NZ]

    def compute(block):
        padded = jnp.pad(block.astype(jnp.float32), ((0, 0), (MARGIN, MARGIN), (0, 0), (0, 0)))
        stacked = jnp.stack([padded[:, tile_index * ZD:tile_index * ZD + TZ] for tile_index in range(tile_total)])
        weighted = network(stacked, first_kernel, second_kernel, head_kernel)
        summed = jnp.zeros((AFF, full_depth, BY, BX), jnp.float32)
        for tile_index in range(tile_total):
            summed = summed.at[:, tile_index * ZD:tile_index * ZD + TZ].add(weighted[tile_index])
        return summed[:, MARGIN:MARGIN + NZ] / coverage[None, :, None, None]

    def skipped(block):
        return jnp.zeros((AFF, NZ, BY, BX), jnp.float32)

    def process_block(paired):
        block, flag = paired
        return lax.cond(flag > 0, compute, skipped, block).astype(jnp.bfloat16)

    return lax.map(process_block, (features, occupied))
```

```python
import functools

import jax
import jax.numpy as jnp
from jax import lax
from jax.experimental import pallas as pl
from jax.experimental.pallas import tpu as pltpu
from jax.sharding import PartitionSpec as P

C = 32
AFF = 3
BLK = 16
BY = 8
BX = 128
ZD = 8
TZ = 12
ROWS = C * BY
TAPS = 3 * ROWS
BLEND = tuple(min(1.0, (t + 0.5) / 4, (TZ - t - 0.5) / 4) for t in range(TZ))
MESH = pl.DeviceIdType.MESH
f32 = jnp.float32
bf16 = jnp.bfloat16


def iota(shape, dim):
    return lax.broadcasted_iota(jnp.int32, shape, dim)


def put_shifted(planes, z, value, first, last):
    base = (z + 1) * TAPS
    value = value.astype(bf16)
    nothing = jnp.zeros_like(value)
    planes[base : base + ROWS, :] = jnp.where(first, nothing, pltpu.roll(value, 1, 1))
    planes[base + ROWS : base + 2 * ROWS, :] = value
    planes[base + 2 * ROWS : base + TAPS, :] = jnp.where(
        last, nothing, pltpu.roll(value, BX - 1, 1)
    )


def conv_pair(planes, weight, pair):
    base = 2 * pair * TAPS
    gathered = jnp.concatenate(
        [planes[base : base + 3 * TAPS, :], planes[base + TAPS : base + 4 * TAPS, :]], axis=1
    )
    return jnp.dot(weight[...], gathered, preferred_element_type=f32)


def tile_network(tile, acts_in, acts_mid, w_one, w_two, w_top, result, low, high):
    lane = iota((ROWS, BX), 1)
    first, last = lane == 0, lane == BX - 1
    sums, acts, logits = {}, {}, {}

    def prepare(p):
        value = tile[:, 16 * p : 16 * p + 16, :].astype(f32).reshape(C, 2, BY, BX)
        put_shifted(acts_in, 2 * p, value[:, 0].reshape(ROWS, BX), first, last)
        put_shifted(acts_in, 2 * p + 1, value[:, 1].reshape(ROWS, BX), first, last)

    def conv_one(p):
        sums[p] = conv_pair(acts_in, w_one, p)

    def relu_one(p):
        value = jnp.maximum(sums.pop(p), 0.0)
        put_shifted(acts_mid, 2 * p, value[:, :BX], first, last)
        put_shifted(acts_mid, 2 * p + 1, value[:, BX:], first, last)

    def conv_two(p):
        base = (2 * p + 1) * TAPS + ROWS
        own = jnp.concatenate(
            [acts_in[base : base + ROWS, :], acts_in[base + TAPS : base + TAPS + ROWS, :]], axis=1
        )
        value = conv_pair(acts_mid, w_two, p) + own.astype(f32)
        acts[p] = jnp.maximum(value, 0.0).astype(bf16)

    def head(p):
        value = jnp.dot(w_top[...], acts.pop(p), preferred_element_type=f32)
        pair = [value[:, :BX] * BLEND[2 * p], value[:, BX:] * BLEND[2 * p + 1]]
        if p == 0:
            low[...] = jnp.concatenate(pair, axis=0).astype(bf16)
        elif p == 5:
            high[...] = jnp.concatenate(pair, axis=0).astype(bf16)
        else:
            result[2 * p - 2] = pair[0]
            result[2 * p - 1] = pair[1]

    prepare(0)
    prepare(1)
    for p in range(9):
        if p < 6:
            conv_one(p)
        if p + 2 < 6:
            prepare(p + 2)
        if p < 6:
            relu_one(p)
        if 0 <= p - 2 < 6:
            conv_two(p - 2)
        if 0 <= p - 3 < 6:
            head(p - 3)


def build_banded(taps, banded):
    spread = (iota((C, ROWS), 1) // BY == iota((C, ROWS), 0)).astype(bf16)
    repeat = (iota((ROWS, C), 0) // BY == iota((ROWS, C), 1)).astype(bf16)
    apart = iota((ROWS, ROWS), 1) % BY - iota((ROWS, ROWS), 0) % BY
    for outer in range(9):
        total = jnp.zeros((ROWS, ROWS), f32)
        for dy in range(3):
            at = (outer * 3 + dy) * C
            wide = jnp.dot(taps[at : at + C, :], spread, preferred_element_type=f32).astype(bf16)
            wide = jnp.dot(repeat, wide, preferred_element_type=f32)
            total = jnp.where(apart == dy - 1, wide, total)
        banded[:, outer * ROWS : (outer + 1) * ROWS] = total.astype(bf16)


def build_head(w_head, banded):
    spread = (iota((C, ROWS), 1) // BY == iota((C, ROWS), 0)).astype(bf16)
    wide = jnp.dot(w_head[...], spread, preferred_element_type=f32)
    wide = jnp.broadcast_to(wide[:, None, :], (AFF, BY, ROWS)).reshape(AFF * BY, ROWS)
    apart = iota((AFF * BY, ROWS), 1) % BY - iota((AFF * BY, ROWS), 0) % BY
    banded[...] = jnp.where(apart == 0, wide, 0.0).astype(bf16)


def kernel(
    slots,
    occupied,
    features,
    taps_one,
    taps_two,
    w_head,
    out,
    held,
    tiles,
    acts_in,
    acts_mid,
    w_one,
    w_two,
    w_top,
    result,
    low,
    high,
    from_upper,
    from_lower,
    finished,
    load_sem,
    halo_send,
    halo_recv,
    edge_send,
    edge_recv,
):
    wide = lax.axis_index("wide")
    level = lax.axis_index("narrow")
    depth = 4
    above = (wide, lax.rem(level + 1, depth))
    below = (wide, lax.rem(level + depth - 1, depth))

    load = pltpu.make_async_copy(features, held, load_sem)
    load.start()
    barrier = pltpu.get_barrier_semaphore()
    for neighbour in (above, below):
        pl.semaphore_signal(barrier, inc=1, device_id=neighbour, device_id_type=MESH)
    pl.semaphore_wait(barrier, 2)

    running = []
    count = jnp.int32(0)
    for b in range(BLK):
        count = count + occupied[b]
        running.append(count)

    def halos(s):
        down = pltpu.make_async_remote_copy(
            src_ref=tiles.at[s, :, 16:32, :],
            dst_ref=tiles.at[s, :, 80:96, :],
            send_sem=halo_send.at[s, 0],
            recv_sem=halo_recv.at[s, 0],
            device_id=below,
            device_id_type=MESH,
        )
        up = pltpu.make_async_remote_copy(
            src_ref=tiles.at[s, :, 64:80, :],
            dst_ref=tiles.at[s, :, 0:16, :],
            send_sem=halo_send.at[s, 1],
            recv_sem=halo_recv.at[s, 1],
            device_id=above,
            device_id_type=MESH,
        )
        return down, up

    def edges(s):
        down = pltpu.make_async_remote_copy(
            src_ref=low.at[s],
            dst_ref=from_upper.at[s],
            send_sem=edge_send.at[s, 0],
            recv_sem=edge_recv.at[s, 0],
            device_id=below,
            device_id_type=MESH,
        )
        up = pltpu.make_async_remote_copy(
            src_ref=high.at[s],
            dst_ref=from_lower.at[s],
            send_sem=edge_send.at[s, 1],
            recv_sem=edge_recv.at[s, 1],
            device_id=above,
            device_id_type=MESH,
        )
        return down, up

    load.wait()

    @pl.loop(0, slots)
    def _(s):
        picked = jnp.int32(0)
        for b in range(BLK):
            picked = picked + (running[b] <= s).astype(jnp.int32)
        picked = jnp.minimum(picked, BLK - 1)
        tiles[s, :, 16:80, :] = held[picked]
        for copy in halos(s):
            copy.start()

    for planes in (acts_in, acts_mid):
        planes[0:TAPS, :] = jnp.zeros((TAPS, BX), bf16)
        planes[(TZ + 1) * TAPS : (TZ + 2) * TAPS, :] = jnp.zeros((TAPS, BX), bf16)
    build_banded(taps_one, w_one)
    build_banded(taps_two, w_two)
    build_head(w_head, w_top)

    @pl.loop(0, slots)
    def _(s):
        for copy in halos(s):
            copy.wait()

        @pl.when(level == 0)
        def _():
            tiles[s, :, 0:16, :] = jnp.zeros((C, 16, BX), bf16)

        @pl.when(level == depth - 1)
        def _():
            tiles[s, :, 80:96, :] = jnp.zeros((C, 16, BX), bf16)

        tile_network(
            tiles.at[s],
            acts_in,
            acts_mid,
            w_one,
            w_two,
            w_top,
            result.at[s],
            low.at[s],
            high.at[s],
        )
        for copy in edges(s):
            copy.start()

    has_lower, has_upper = level > 0, level < depth - 1

    @pl.loop(0, slots)
    def _(s):
        for copy in edges(s):
            copy.wait()
        planes = [result[s, z] for z in range(ZD)]
        lower = from_lower[s].astype(f32)
        upper = from_upper[s].astype(f32)
        for i in range(2):
            part = lower[24 * i : 24 * i + 24]
            planes[i] = jnp.where(has_lower, planes[i] + part, planes[i] / BLEND[2 + i])
            part = upper[24 * i : 24 * i + 24]
            planes[6 + i] = jnp.where(has_upper, planes[6 + i] + part, planes[6 + i] / BLEND[8 + i])
        for a in range(AFF):
            for p in range(4):
                two = [planes[2 * p + i][BY * a : BY * a + BY] for i in range(2)]
                finished[s, a, 16 * p : 16 * p + 16, :] = jnp.concatenate(two, axis=0).astype(bf16)

    for b in range(BLK):
        kept = finished[running[b] - occupied[b]]
        out[b] = jnp.where(occupied[b] > 0, kept, jnp.zeros_like(kept))


def on_device(features, occupied, w_first, w_second, w_head):
    slots = BLK
    stacked = jnp.stack([w_first, w_second])
    taps = jnp.transpose(stacked, (0, 3, 5, 4, 1, 2)).reshape(2, 27 * C, C)
    vmem = pl.BlockSpec(memory_space=pltpu.VMEM)
    call = pl.pallas_call(
        functools.partial(kernel, slots),
        out_shape=jax.ShapeDtypeStruct((BLK, AFF, ZD * BY, BX), bf16),
        in_specs=[
            pl.BlockSpec(memory_space=pltpu.SMEM),
            pl.BlockSpec(memory_space=pl.ANY),
            vmem,
            vmem,
            vmem,
        ],
        out_specs=vmem,
        scratch_shapes=[
            pltpu.VMEM((BLK, C, ZD * BY, BX), bf16),
            pltpu.VMEM((slots, C, TZ * BY, BX), bf16),
            pltpu.VMEM(((TZ + 2) * TAPS, BX), bf16),
            pltpu.VMEM(((TZ + 2) * TAPS, BX), bf16),
            pltpu.VMEM((ROWS, 9 * ROWS), bf16),
            pltpu.VMEM((ROWS, 9 * ROWS), bf16),
            pltpu.VMEM((AFF * BY, ROWS), bf16),
            pltpu.VMEM((slots, ZD, AFF * BY, BX), f32),
            pltpu.VMEM((slots, 2 * AFF * BY, BX), bf16),
            pltpu.VMEM((slots, 2 * AFF * BY, BX), bf16),
            pltpu.VMEM((slots, 2 * AFF * BY, BX), bf16),
            pltpu.VMEM((slots, 2 * AFF * BY, BX), bf16),
            pltpu.VMEM((slots, AFF, ZD * BY, BX), bf16),
            pltpu.SemaphoreType.DMA,
            pltpu.SemaphoreType.DMA((slots, 2)),
            pltpu.SemaphoreType.DMA((slots, 2)),
            pltpu.SemaphoreType.DMA((slots, 2)),
            pltpu.SemaphoreType.DMA((slots, 2)),
        ],
        compiler_params=pltpu.CompilerParams(
            collective_id=0, has_side_effects=True, vmem_limit_bytes=56 << 20
        ),
    )
    out = call(
        occupied, features.reshape(BLK, C, ZD * BY, BX), taps[0], taps[1], w_head
    )
    return out.reshape(BLK, AFF, ZD, BY, BX)


def solution(mesh):
    in_specs = (P("wide", None, "narrow", None, None), P("wide"), P(), P(), P())
    out_specs = P("wide", None, "narrow", None, None)
    return jax.shard_map(
        on_device, mesh=mesh, in_specs=in_specs, out_specs=out_specs, check_vma=False
    )
```

```python
import functools

import jax
import jax.numpy as jnp
from jax import lax
from jax.experimental import pallas as pl
from jax.experimental.pallas import tpu as pltpu
from jax.sharding import PartitionSpec as P

C = 32
AFF = 3
BLK = 16
BY = 8
BX = 128
ZD = 8
TZ = 12
ROWS = C * BY
TAPS = 3 * ROWS
BLEND = tuple(min(1.0, (t + 0.5) / 4, (TZ - t - 0.5) / 4) for t in range(TZ))
MESH = pl.DeviceIdType.MESH
f32 = jnp.float32
bf16 = jnp.bfloat16


def iota(shape, dim):
    return lax.broadcasted_iota(jnp.int32, shape, dim)


def put_shifted(planes, z, value, first, last):
    base = (z + 1) * TAPS
    value = value.astype(bf16)
    nothing = jnp.zeros_like(value)
    planes[base : base + ROWS, :] = jnp.where(first, nothing, pltpu.roll(value, 1, 1))
    planes[base + ROWS : base + 2 * ROWS, :] = value
    planes[base + 2 * ROWS : base + TAPS, :] = jnp.where(
        last, nothing, pltpu.roll(value, BX - 1, 1)
    )


def conv_pair(planes, weight, pair):
    base = 2 * pair * TAPS
    gathered = jnp.concatenate(
        [planes[base : base + 3 * TAPS, :], planes[base + TAPS : base + 4 * TAPS, :]], axis=1
    )
    return jnp.dot(weight[...], gathered, preferred_element_type=f32)


def tile_network(tile, acts_in, acts_mid, w_one, w_two, w_top, result, low, high):
    lane = iota((ROWS, BX), 1)
    first, last = lane == 0, lane == BX - 1
    sums, acts, logits = {}, {}, {}

    def prepare(p):
        value = tile[:, 16 * p : 16 * p + 16, :].astype(f32).reshape(C, 2, BY, BX)
        put_shifted(acts_in, 2 * p, value[:, 0].reshape(ROWS, BX), first, last)
        put_shifted(acts_in, 2 * p + 1, value[:, 1].reshape(ROWS, BX), first, last)

    def conv_one(p):
        sums[p] = conv_pair(acts_in, w_one, p)

    def relu_one(p):
        value = jnp.maximum(sums.pop(p), 0.0)
        put_shifted(acts_mid, 2 * p, value[:, :BX], first, last)
        put_shifted(acts_mid, 2 * p + 1, value[:, BX:], first, last)

    def conv_two(p):
        base = (2 * p + 1) * TAPS + ROWS
        own = jnp.concatenate(
            [acts_in[base : base + ROWS, :], acts_in[base + TAPS : base + TAPS + ROWS, :]], axis=1
        )
        value = conv_pair(acts_mid, w_two, p) + own.astype(f32)
        acts[p] = jnp.maximum(value, 0.0).astype(bf16)

    def head(p):
        value = jnp.dot(w_top[...], acts.pop(p), preferred_element_type=f32)
        pair = [value[:, :BX] * BLEND[2 * p], value[:, BX:] * BLEND[2 * p + 1]]
        if p == 0:
            low[...] = jnp.concatenate(pair, axis=0).astype(bf16)
        elif p == 5:
            high[...] = jnp.concatenate(pair, axis=0).astype(bf16)
        else:
            result[2 * p - 2] = pair[0]
            result[2 * p - 1] = pair[1]

    prepare(0)
    prepare(1)
    for p in range(9):
        if p < 6:
            conv_one(p)
        if p + 2 < 6:
            prepare(p + 2)
        if p < 6:
            relu_one(p)
        if 0 <= p - 2 < 6:
            conv_two(p - 2)
        if 0 <= p - 3 < 6:
            head(p - 3)


def build_banded(taps, banded):
    spread = (iota((C, ROWS), 1) // BY == iota((C, ROWS), 0)).astype(bf16)
    repeat = (iota((ROWS, C), 0) // BY == iota((ROWS, C), 1)).astype(bf16)
    apart = iota((ROWS, ROWS), 1) % BY - iota((ROWS, ROWS), 0) % BY
    for outer in range(9):
        total = jnp.zeros((ROWS, ROWS), f32)
        for dy in range(3):
            at = ((outer // 3 * 3 + dy) * 3 + outer % 3) * C
            wide = jnp.dot(taps[at : at + C, :], spread, preferred_element_type=f32).astype(bf16)
            wide = jnp.dot(repeat, wide, preferred_element_type=f32)
            total = jnp.where(apart == dy - 1, wide, total)
        banded[:, outer * ROWS : (outer + 1) * ROWS] = total.astype(bf16)


def build_head(w_head, banded):
    spread = (iota((C, ROWS), 1) // BY == iota((C, ROWS), 0)).astype(bf16)
    wide = jnp.dot(w_head[...], spread, preferred_element_type=f32)
    wide = jnp.broadcast_to(wide[:, None, :], (AFF, BY, ROWS)).reshape(AFF * BY, ROWS)
    apart = iota((AFF * BY, ROWS), 1) % BY - iota((AFF * BY, ROWS), 0) % BY
    banded[...] = jnp.where(apart == 0, wide, 0.0).astype(bf16)


DEPTH = 4


def running_counts(occupied):
    running = []
    count = jnp.int32(0)
    for b in range(BLK):
        count = count + occupied[b]
        running.append(count)
    return running


def block_of_rank(running, rank):
    picked = jnp.int32(0)
    for b in range(BLK):
        picked = picked + jnp.where(running[b] <= rank, 1, 0)
    return jnp.minimum(picked, BLK - 1)


def halo_copies(tiles, send, recv, above, below, s):
    down = pltpu.make_async_remote_copy(
        src_ref=tiles.at[s, :, 16:32, :],
        dst_ref=tiles.at[s, :, 80:96, :],
        send_sem=send.at[s, 0],
        recv_sem=recv.at[s, 0],
        device_id=below,
        device_id_type=MESH,
    )
    up = pltpu.make_async_remote_copy(
        src_ref=tiles.at[s, :, 64:80, :],
        dst_ref=tiles.at[s, :, 0:16, :],
        send_sem=send.at[s, 1],
        recv_sem=recv.at[s, 1],
        device_id=above,
        device_id_type=MESH,
    )
    return down, up


def edge_copies(low, high, from_upper, from_lower, send, recv, above, below, s):
    down = pltpu.make_async_remote_copy(
        src_ref=low.at[s],
        dst_ref=from_upper.at[s],
        send_sem=send.at[s, 0],
        recv_sem=recv.at[s, 0],
        device_id=below,
        device_id_type=MESH,
    )
    up = pltpu.make_async_remote_copy(
        src_ref=high.at[s],
        dst_ref=from_lower.at[s],
        send_sem=send.at[s, 1],
        recv_sem=recv.at[s, 1],
        device_id=above,
        device_id_type=MESH,
    )
    return down, up


def clear_outside(tiles, s, level):
    @pl.when(level == 0)
    def _():
        tiles[s, :, 0:16, :] = jnp.zeros((C, 16, BX), bf16)

    @pl.when(level == DEPTH - 1)
    def _():
        tiles[s, :, 80:96, :] = jnp.zeros((C, 16, BX), bf16)


def finish(result, from_lower, from_upper, finished, s, level):
    has_lower, has_upper = level > 0, level < DEPTH - 1
    planes = [result[s, z] for z in range(ZD)]
    lower = from_lower[s].astype(f32)
    upper = from_upper[s].astype(f32)
    for i in range(2):
        part = lower[24 * i : 24 * i + 24]
        planes[i] = jnp.where(has_lower, planes[i] + part, planes[i] / BLEND[2 + i])
        part = upper[24 * i : 24 * i + 24]
        planes[6 + i] = jnp.where(has_upper, planes[6 + i] + part, planes[6 + i] / BLEND[8 + i])
    for a in range(AFF):
        for p in range(4):
            two = [planes[2 * p + i][BY * a : BY * a + BY] for i in range(2)]
            finished[s, a, 16 * p : 16 * p + 16, :] = jnp.concatenate(two, axis=0).astype(bf16)


def whole_kernel(
    slots,
    occupied,
    features,
    taps_one,
    taps_two,
    w_head,
    out,
    held,
    tiles,
    acts_in,
    acts_mid,
    w_one,
    w_two,
    w_top,
    result,
    low,
    high,
    from_upper,
    from_lower,
    finished,
    load_sem,
    halo_send,
    halo_recv,
    edge_send,
    edge_recv,
):
    wide = lax.axis_index("wide")
    level = lax.axis_index("narrow")
    above = (wide, lax.rem(level + 1, DEPTH))
    below = (wide, lax.rem(level + DEPTH - 1, DEPTH))

    load = pltpu.make_async_copy(features, held, load_sem)
    load.start()
    barrier = pltpu.get_barrier_semaphore()
    for neighbour in (above, below):
        pl.semaphore_signal(barrier, inc=1, device_id=neighbour, device_id_type=MESH)
    pl.semaphore_wait(barrier, 2)

    running = running_counts(occupied)
    halos = functools.partial(halo_copies, tiles, halo_send, halo_recv, above, below)
    edges = functools.partial(
        edge_copies, low, high, from_upper, from_lower, edge_send, edge_recv, above, below
    )
    load.wait()

    @pl.loop(0, slots)
    def _(s):
        tiles[s, :, 16:80, :] = held[block_of_rank(running, s)]
        for copy in halos(s):
            copy.start()

    for planes in (acts_in, acts_mid):
        planes[0:TAPS, :] = jnp.zeros((TAPS, BX), bf16)
        planes[(TZ + 1) * TAPS : (TZ + 2) * TAPS, :] = jnp.zeros((TAPS, BX), bf16)
    build_banded(taps_one, w_one)
    build_banded(taps_two, w_two)
    build_head(w_head, w_top)

    @pl.loop(0, slots)
    def _(s):
        for copy in halos(s):
            copy.wait()
        clear_outside(tiles, s, level)
        tile_network(
            tiles.at[s],
            acts_in,
            acts_mid,
            w_one,
            w_two,
            w_top,
            result.at[s],
            low.at[s],
            high.at[s],
        )
        for copy in edges(s):
            copy.start()

    @pl.loop(0, slots)
    def _(s):
        for copy in edges(s):
            copy.wait()
        finish(result, from_lower, from_upper, finished, s, level)

    for b in range(BLK):
        kept = finished[running[b] - occupied[b]]
        out[b] = jnp.where(occupied[b] > 0, kept, jnp.zeros_like(kept))


SLOTS = 7
SURE = 3
LATE = 5
TARGET = 5
TWINS = 3
EARLY = TWINS + 4
LANES = EARLY + 2
COLUMNS = 32


def lane_columns(lane, sign):
    column = lax.axis_index("wide")
    core, y, x = column % 2, column // 2 % 4, column // 8
    if lane < TWINS:
        return column + 1 - 2 * core
    if lane < EARLY:
        step = sign * (1, -1, 1, -1)[lane - TWINS] + 4
        if lane < TWINS + 2:
            x = (x + step) % 4
        else:
            y = (y + step) % 4
        return (x * 4 + y) * 2 + core
    step = sign * (1, -1)[lane - EARLY]
    along_x = 1 - core if sign > 0 else core
    x = (x + step * along_x + 4) % 4
    y = (y + step * (1 - along_x) + 4) % 4
    return (x * 4 + y) * 2 + 1 - core


def turned(value, dim, step):
    step = step % 4
    if step == 0:
        return value
    head = lax.slice_in_dim(value, 0, step, axis=dim)
    return jnp.concatenate([lax.slice_in_dim(value, step, 4, axis=dim), head], axis=dim)


def other_core(value):
    return jnp.concatenate([value[:, :, 1:2], value[:, :, 0:1]], axis=2)


def across(value, lane, sign):
    if lane < TWINS:
        return other_core(value)
    if lane < EARLY:
        step = sign * (1, -1, 1, -1)[lane - TWINS]
        return turned(value, 0 if lane < TWINS + 2 else 1, step)
    step = sign * (1, -1)[lane - EARLY]
    flipped = other_core(value)
    over_x, over_y = turned(flipped, 0, step), turned(flipped, 1, step)
    pair = (over_x, over_y) if sign > 0 else (over_y, over_x)
    return jnp.concatenate([pair[0][:, :, 0:1], pair[1][:, :, 1:2]], axis=2)


def make_plan(counts, used):
    load = counts
    own = counts
    for turn in range(3):
        for lane in range(LANES):
            there = across(load, lane, 1)
            sends = (load > TARGET) & (load - there >= 2) & (own > 0)
            if turn == 0:
                sends = sends & (there < TARGET)
            else:
                sends = sends & (used[lane].reshape(load.shape) == 0)
            sends = jnp.where(sends, 1, 0)
            if turn == 0:
                used[lane] = sends.reshape(used.shape[1:])
            else:
                used[lane] = used[lane] + sends.reshape(used.shape[1:])
            own = own - sends
            load = load - sends + across(sends, lane, -1)
    early = jnp.zeros_like(load)
    late = jnp.zeros_like(load)
    for lane in range(LANES):
        taken = across(used[lane].reshape(load.shape), lane, -1)
        if lane < EARLY:
            early = early + taken
        else:
            late = late + taken
    need = jnp.maximum(own, SURE) + early
    need = jnp.where(late > 0, jnp.maximum(need, LATE) + late, need)
    return jnp.max(need.reshape((COLUMNS,) + need.shape[3:]), axis=0)


def shared_kernel(
    occupied,
    features,
    taps_one,
    taps_two,
    w_head,
    out,
    needed,
    held,
    tiles,
    acts_in,
    acts_mid,
    w_one,
    w_two,
    w_top,
    result,
    low,
    high,
    from_upper,
    from_lower,
    finished,
    mine,
    counts,
    used,
    early_out,
    early_in,
    late_out,
    late_in,
    back_out,
    back_in,
    load_sem,
    count_send,
    count_recv,
    lane_send,
    lane_recv,
    back_send,
    back_recv,
    halo_send,
    halo_recv,
    edge_send,
    edge_recv,
):
    wide = lax.axis_index("wide")
    level = lax.axis_index("narrow")
    above = (wide, lax.rem(level + 1, DEPTH))
    below = (wide, lax.rem(level + DEPTH - 1, DEPTH))

    load = pltpu.make_async_copy(features, held, load_sem)
    load.start()
    barrier = pltpu.get_barrier_semaphore()
    for neighbour in (above, below):
        pl.semaphore_signal(barrier, inc=1, device_id=neighbour, device_id_type=MESH)

    @pl.loop(1, COLUMNS)
    def _(o):
        pl.semaphore_signal(
            barrier,
            inc=1,
            device_id=(lax.rem(wide + o, COLUMNS), level),
            device_id_type=MESH,
        )

    running = running_counts(occupied)
    held_blocks = running[-1]
    mine[...] = jnp.full(mine.shape, held_blocks, jnp.int32)
    counts[wide] = mine[...]
    pl.semaphore_wait(barrier, COLUMNS + 1)

    def count_copy(o):
        return pltpu.make_async_remote_copy(
            src_ref=mine,
            dst_ref=counts.at[wide],
            send_sem=count_send.at[o],
            recv_sem=count_recv.at[o],
            device_id=(lax.rem(wide + o, COLUMNS), level),
            device_id_type=MESH,
        )

    @pl.loop(1, COLUMNS)
    def _(o):
        count_copy(o).start()

    def lane_copy(lane):
        if lane < EARLY:
            source, target = early_out.at[lane], early_in.at[lane]
        else:
            source, target = late_out.at[lane - EARLY], late_in.at[lane - EARLY]
        return pltpu.make_async_remote_copy(
            src_ref=source,
            dst_ref=target,
            send_sem=lane_send.at[lane],
            recv_sem=lane_recv.at[lane],
            device_id=(lane_columns(lane, 1), level),
            device_id_type=MESH,
        )

    def back_copy(lane):
        return pltpu.make_async_remote_copy(
            src_ref=back_out.at[lane],
            dst_ref=back_in.at[lane],
            send_sem=back_send.at[lane],
            recv_sem=back_recv.at[lane],
            device_id=(lane_columns(lane, -1), level),
            device_id_type=MESH,
        )

    halos = functools.partial(halo_copies, tiles, halo_send, halo_recv, above, below)
    edges = functools.partial(
        edge_copies, low, high, from_upper, from_lower, edge_send, edge_recv, above, below
    )

    build_banded(taps_one, w_one)
    load.wait()
    for s in range(SURE):
        tiles[s, :, 16:80, :] = held[block_of_rank(running, s)]
        for copy in halos(s):
            copy.start()

    @pl.loop(1, COLUMNS)
    def _(o):
        count_copy(o).wait()

    tile_shape = (4, 4, 2) + counts.shape[1:]
    needed[...] = make_plan(counts[...].reshape(tile_shape), used)

    sent, taken = [], []
    for lane in range(LANES):
        sent.append(used[lane, wide, 0, 0])
        taken.append(used[lane, lane_columns(lane, -1), 0, 0])
    kept = held_blocks - sum(sent)
    ranks = []
    rank = kept
    for lane in range(LANES):
        ranks.append(rank)
        rank = rank + sent[lane]
    places = []
    place = jnp.maximum(kept, SURE)
    for lane in range(LANES):
        if lane == EARLY:
            place = jnp.maximum(place, LATE)
        places.append(place)
        place = place + taken[lane]

    for lane in range(EARLY):
        early_out[lane] = held[block_of_rank(running, ranks[lane])]
        lane_copy(lane).start()

    for planes in (acts_in, acts_mid):
        planes[0:TAPS, :] = jnp.zeros((TAPS, BX), bf16)
        planes[(TZ + 1) * TAPS : (TZ + 2) * TAPS, :] = jnp.zeros((TAPS, BX), bf16)
    build_banded(taps_two, w_two)
    build_head(w_head, w_top)

    def stage(s):
        own = held[block_of_rank(running, s)]
        chosen = jnp.int32(0)
        for lane in range(EARLY):
            chosen = chosen + jnp.where((taken[lane] > 0) & (places[lane] == s), lane, 0)
        value = jnp.where(s < kept, own, early_in[chosen])
        if s >= LATE:
            chosen, found = jnp.int32(0), jnp.int32(0)
            for lane in range(EARLY, LANES):
                here = (taken[lane] > 0) & (places[lane] == s)
                chosen = chosen + jnp.where(here, lane - EARLY, 0)
                found = found + jnp.where(here, 1, 0)
            value = jnp.where(found > 0, late_in[chosen], value)
        tiles[s, :, 16:80, :] = value
        for copy in halos(s):
            copy.start()

    @pl.loop(0, SLOTS)
    def _(s):
        @pl.when(s == 1)
        def _():
            for lane in range(EARLY, LANES):
                late_out[lane - EARLY] = held[block_of_rank(running, ranks[lane])]
                lane_copy(lane).start()

        @pl.when(s == SURE - 1)
        def _():
            for lane in range(EARLY):
                lane_copy(lane).wait()
            for later in range(SURE, LATE):
                stage(later)

        @pl.when(s == LATE - 1)
        def _():
            for lane in range(EARLY, LANES):
                lane_copy(lane).wait()
            for later in range(LATE, SLOTS):
                stage(later)

        for copy in halos(s):
            copy.wait()
        clear_outside(tiles, s, level)
        tile_network(
            tiles.at[s],
            acts_in,
            acts_mid,
            w_one,
            w_two,
            w_top,
            result.at[s],
            low.at[s],
            high.at[s],
        )
        for copy in edges(s):
            copy.start()

    @pl.loop(0, SLOTS)
    def _(s):
        for copy in edges(s):
            copy.wait()
        finish(result, from_lower, from_upper, finished, s, level)

    for lane in range(LANES):
        back_out[lane] = finished[jnp.clip(places[lane], 0, SLOTS - 1)]
        back_copy(lane).start()
    for lane in range(LANES):
        back_copy(lane).wait()

    for b in range(BLK):
        rank = running[b] - occupied[b]
        chosen = jnp.int32(0)
        for lane in range(LANES):
            chosen = chosen + jnp.where((sent[lane] > 0) & (ranks[lane] == rank), lane, 0)
        local = finished[jnp.minimum(rank, SLOTS - 1)]
        value = jnp.where(rank < kept, local, back_in[chosen])
        out[b] = jnp.where(occupied[b] > 0, value, jnp.zeros_like(value))


def work_scratch(slots):
    return [
        pltpu.VMEM((BLK, C, ZD * BY, BX), bf16),
        pltpu.VMEM((slots, C, TZ * BY, BX), bf16),
        pltpu.VMEM(((TZ + 2) * TAPS, BX), bf16),
        pltpu.VMEM(((TZ + 2) * TAPS, BX), bf16),
        pltpu.VMEM((ROWS, 9 * ROWS), bf16),
        pltpu.VMEM((ROWS, 9 * ROWS), bf16),
        pltpu.VMEM((AFF * BY, ROWS), bf16),
        pltpu.VMEM((slots, ZD, AFF * BY, BX), f32),
        pltpu.VMEM((slots, 2 * AFF * BY, BX), bf16),
        pltpu.VMEM((slots, 2 * AFF * BY, BX), bf16),
        pltpu.VMEM((slots, 2 * AFF * BY, BX), bf16),
        pltpu.VMEM((slots, 2 * AFF * BY, BX), bf16),
        pltpu.VMEM((slots, AFF, ZD * BY, BX), bf16),
    ]


def on_device(features, occupied, w_first, w_second, w_head):
    vmem = pl.BlockSpec(memory_space=pltpu.VMEM)
    in_specs = [
        pl.BlockSpec(memory_space=pltpu.SMEM),
        pl.BlockSpec(memory_space=pl.ANY),
        vmem,
        vmem,
        vmem,
    ]
    affinities = jax.ShapeDtypeStruct((BLK, AFF, ZD * BY, BX), bf16)
    dma = pltpu.SemaphoreType.DMA
    shared = pl.pallas_call(
        shared_kernel,
        out_shape=[affinities, jax.ShapeDtypeStruct((8, 128), jnp.int32)],
        in_specs=in_specs,
        out_specs=[vmem, vmem],
        scratch_shapes=work_scratch(SLOTS)
        + [
            pltpu.VMEM((8, 128), jnp.int32),
            pltpu.VMEM((COLUMNS, 8, 128), jnp.int32),
            pltpu.VMEM((LANES, COLUMNS, 8, 128), jnp.int32),
            pltpu.VMEM((EARLY, C, ZD * BY, BX), bf16),
            pltpu.VMEM((EARLY, C, ZD * BY, BX), bf16),
            pltpu.VMEM((LANES - EARLY, C, ZD * BY, BX), bf16),
            pltpu.VMEM((LANES - EARLY, C, ZD * BY, BX), bf16),
            pltpu.VMEM((LANES, AFF, ZD * BY, BX), bf16),
            pltpu.VMEM((LANES, AFF, ZD * BY, BX), bf16),
            dma,
            dma((COLUMNS,)),
            dma((COLUMNS,)),
            dma((LANES,)),
            dma((LANES,)),
            dma((LANES,)),
            dma((LANES,)),
            dma((SLOTS, 2)),
            dma((SLOTS, 2)),
            dma((SLOTS, 2)),
            dma((SLOTS, 2)),
        ],
        compiler_params=pltpu.CompilerParams(
            collective_id=0, has_side_effects=True, vmem_limit_bytes=56 << 20
        ),
    )
    whole = pl.pallas_call(
        functools.partial(whole_kernel, BLK),
        out_shape=affinities,
        in_specs=in_specs,
        out_specs=vmem,
        scratch_shapes=work_scratch(BLK)
        + [dma, dma((BLK, 2)), dma((BLK, 2)), dma((BLK, 2)), dma((BLK, 2))],
        compiler_params=pltpu.CompilerParams(
            collective_id=1, has_side_effects=True, vmem_limit_bytes=56 << 20
        ),
    )
    taps = [
        jnp.transpose(w, (2, 3, 4, 0, 1)).reshape(27 * C, C) for w in (w_first, w_second)
    ]
    args = (occupied, features.reshape(BLK, C, ZD * BY, BX), *taps, w_head)
    out, needed = shared(*args)
    out = lax.cond(needed[0, 0] > SLOTS, lambda: whole(*args), lambda: out)
    return out.reshape(BLK, AFF, ZD, BY, BX)


def solution(mesh):
    in_specs = (P("wide", None, "narrow", None, None), P("wide"), P(), P(), P())
    out_specs = P("wide", None, "narrow", None, None)
    return jax.shard_map(
        on_device, mesh=mesh, in_specs=in_specs, out_specs=out_specs, check_vma=False
    )
```

```python
import functools

import jax
import jax.numpy as jnp
from jax import lax
from jax.experimental import pallas as pl
from jax.experimental.pallas import tpu as pltpu
from jax.sharding import PartitionSpec as P

C = 32
AFF = 3
BLK = 16
BY = 8
BX = 128
ZD = 8
TZ = 12
ROWS = C * BY
TAPS = 3 * ROWS
BLEND = tuple(min(1.0, (t + 0.5) / 4, (TZ - t - 0.5) / 4) for t in range(TZ))
MESH = pl.DeviceIdType.MESH
f32 = jnp.float32
bf16 = jnp.bfloat16


def iota(shape, dim):
    return lax.broadcasted_iota(jnp.int32, shape, dim)


def put_shifted(planes, z, value, first, last):
    base = (z + 1) * TAPS
    value = value.astype(bf16)
    nothing = jnp.zeros_like(value)
    planes[base : base + ROWS, :] = jnp.where(first, nothing, pltpu.roll(value, 1, 1))
    planes[base + ROWS : base + 2 * ROWS, :] = value
    planes[base + 2 * ROWS : base + TAPS, :] = jnp.where(
        last, nothing, pltpu.roll(value, BX - 1, 1)
    )


def conv_pair(planes, weight, pair):
    base = 2 * pair * TAPS
    gathered = jnp.concatenate(
        [planes[base : base + 3 * TAPS, :], planes[base + TAPS : base + 4 * TAPS, :]], axis=1
    )
    return jnp.dot(weight[...], gathered, preferred_element_type=f32)


def work_through(
    slots,
    level,
    tiles,
    acts_in,
    acts_mid,
    w_one,
    w_two,
    w_top,
    result,
    low,
    high,
    finished,
    from_lower,
    from_upper,
    halos,
    edges,
    before,
):
    lane = iota((ROWS, BX), 1)
    first, last = lane == 0, lane == BX - 1

    def prepare(s, p):
        value = tiles[s, :, 16 * p : 16 * p + 16, :].astype(f32)
        if p == 0:
            value = jnp.where(level > 0, value, 0.0)
        if p == 5:
            value = jnp.where(level < DEPTH - 1, value, 0.0)
        value = value.reshape(C, 2, BY, BX)
        put_shifted(acts_in, 2 * p, value[:, 0].reshape(ROWS, BX), first, last)
        put_shifted(acts_in, 2 * p + 1, value[:, 1].reshape(ROWS, BX), first, last)

    def conv_one(p):
        value = jnp.maximum(conv_pair(acts_in, w_one, p), 0.0)
        put_shifted(acts_mid, 2 * p, value[:, :BX], first, last)
        put_shifted(acts_mid, 2 * p + 1, value[:, BX:], first, last)

    def conv_two(p):
        base = (2 * p + 1) * TAPS + ROWS
        own = jnp.concatenate(
            [acts_in[base : base + ROWS, :], acts_in[base + TAPS : base + TAPS + ROWS, :]], axis=1
        )
        value = conv_pair(acts_mid, w_two, p) + own.astype(f32)
        return jnp.maximum(value, 0.0).astype(bf16)

    def head(s, p, acts):
        value = jnp.dot(w_top[...], acts, preferred_element_type=f32)
        pair = [value[:, :BX] * BLEND[2 * p], value[:, BX:] * BLEND[2 * p + 1]]
        if p == 0:
            low[s] = jnp.concatenate(pair, axis=0).astype(bf16)
        elif p == 5:
            high[s] = jnp.concatenate(pair, axis=0).astype(bf16)
        else:
            result[s, 2 * p - 2] = pair[0]
            result[s, 2 * p - 1] = pair[1]

    def close(s):
        for copy in edges(s):
            copy.wait()
        finish(result, from_lower, from_upper, finished, s, level)

    for copy in halos(0):
        copy.wait()
    prepare(0, 0)
    prepare(0, 1)

    @pl.loop(0, slots)
    def _(s):
        before(s)
        previous = jnp.maximum(s - 1, 0)
        conv_one(0)
        prepare(s, 2)
        acts_4 = conv_two(4)
        conv_one(1)
        prepare(s, 3)
        head(previous, 4, acts_4)
        acts_5 = conv_two(5)
        conv_one(2)
        prepare(s, 4)
        head(previous, 5, acts_5)
        acts_0 = conv_two(0)
        conv_one(3)
        prepare(s, 5)
        acts_1 = conv_two(1)
        head(s, 0, acts_0)
        conv_one(4)
        acts_2 = conv_two(2)
        head(s, 1, acts_1)
        conv_one(5)

        @pl.when(s > 0)
        def _():
            for copy in edges(s - 1):
                copy.start()

        @pl.when(s < slots - 1)
        def _():
            for copy in halos(s + 1):
                copy.wait()

        following = jnp.minimum(s + 1, slots - 1)
        acts_3 = conv_two(3)
        head(s, 2, acts_2)
        prepare(following, 0)
        prepare(following, 1)
        head(s, 3, acts_3)

        @pl.when(s > 1)
        def _():
            close(s - 2)

    acts_4 = conv_two(4)
    acts_5 = conv_two(5)
    head(slots - 1, 4, acts_4)
    head(slots - 1, 5, acts_5)
    for copy in edges(slots - 1):
        copy.start()
    close(slots - 2)
    close(slots - 1)


def build_banded(taps, mixed, banded):
    blocks = []
    for outer in range(9):
        rows = [((outer // 3 * 3 + dy) * 3 + outer % 3) * C for dy in range(3)]
        blocks.append(
            jnp.concatenate([taps[at : at + C, :].astype(f32) for at in rows], axis=1)
        )
    stacked = jnp.concatenate(blocks, axis=0).astype(bf16)
    row, col = iota((3 * C, ROWS), 0), iota((3 * C, ROWS), 1)
    same = row % C == col // BY
    for y in range(BY):
        spread = (same & (col % BY == y + row // C - 1)).astype(bf16)
        wide = jnp.dot(stacked, spread, preferred_element_type=f32).astype(bf16)
        for outer in range(9):
            mixed[y * C : (y + 1) * C, outer * ROWS : (outer + 1) * ROWS] = wide[
                outer * C : (outer + 1) * C
            ]
    row, col = iota((ROWS, ROWS), 0), iota((ROWS, ROWS), 1)
    order = ((row // BY == col % C) & (row % BY == col // C)).astype(bf16)
    for outer in range(9):
        cut = slice(outer * ROWS, (outer + 1) * ROWS)
        banded[:, cut] = jnp.dot(order, mixed[:, cut], preferred_element_type=f32).astype(bf16)


def build_head(w_head, banded):
    spread = (iota((C, ROWS), 1) // BY == iota((C, ROWS), 0)).astype(bf16)
    wide = jnp.dot(w_head[...], spread, preferred_element_type=f32)
    wide = jnp.broadcast_to(wide[:, None, :], (AFF, BY, ROWS)).reshape(AFF * BY, ROWS)
    apart = iota((AFF * BY, ROWS), 1) % BY - iota((AFF * BY, ROWS), 0) % BY
    banded[...] = jnp.where(apart == 0, wide, 0.0).astype(bf16)


DEPTH = 4


def running_counts(occupied):
    running = []
    count = jnp.int32(0)
    for b in range(BLK):
        count = count + occupied[b]
        running.append(count)
    return running


def block_of_rank(running, rank):
    picked = jnp.int32(0)
    for b in range(BLK):
        picked = picked + jnp.where(running[b] <= rank, 1, 0)
    return jnp.minimum(picked, BLK - 1)


def halo_copies(tiles, send, recv, above, below, s):
    down = pltpu.make_async_remote_copy(
        src_ref=tiles.at[s, :, 16:32, :],
        dst_ref=tiles.at[s, :, 80:96, :],
        send_sem=send.at[s, 0],
        recv_sem=recv.at[s, 0],
        device_id=below,
        device_id_type=MESH,
    )
    up = pltpu.make_async_remote_copy(
        src_ref=tiles.at[s, :, 64:80, :],
        dst_ref=tiles.at[s, :, 0:16, :],
        send_sem=send.at[s, 1],
        recv_sem=recv.at[s, 1],
        device_id=above,
        device_id_type=MESH,
    )
    return down, up


def edge_copies(low, high, from_upper, from_lower, send, recv, above, below, s):
    down = pltpu.make_async_remote_copy(
        src_ref=low.at[s],
        dst_ref=from_upper.at[s],
        send_sem=send.at[s, 0],
        recv_sem=recv.at[s, 0],
        device_id=below,
        device_id_type=MESH,
    )
    up = pltpu.make_async_remote_copy(
        src_ref=high.at[s],
        dst_ref=from_lower.at[s],
        send_sem=send.at[s, 1],
        recv_sem=recv.at[s, 1],
        device_id=above,
        device_id_type=MESH,
    )
    return down, up


def finish(result, from_lower, from_upper, finished, s, level):
    has_lower, has_upper = level > 0, level < DEPTH - 1
    planes = [result[s, z] for z in range(ZD)]
    lower = from_lower[s].astype(f32)
    upper = from_upper[s].astype(f32)
    for i in range(2):
        part = lower[24 * i : 24 * i + 24]
        planes[i] = jnp.where(has_lower, planes[i] + part, planes[i] / BLEND[2 + i])
        part = upper[24 * i : 24 * i + 24]
        planes[6 + i] = jnp.where(has_upper, planes[6 + i] + part, planes[6 + i] / BLEND[8 + i])
    for a in range(AFF):
        for p in range(4):
            two = [planes[2 * p + i][BY * a : BY * a + BY] for i in range(2)]
            finished[s, a, 16 * p : 16 * p + 16, :] = jnp.concatenate(two, axis=0).astype(bf16)


def whole_kernel(
    slots,
    occupied,
    features,
    taps_one,
    taps_two,
    w_head,
    out,
    held,
    tiles,
    acts_in,
    acts_mid,
    w_one,
    w_two,
    w_top,
    mixed,
    result,
    low,
    high,
    from_upper,
    from_lower,
    finished,
    load_sem,
    halo_send,
    halo_recv,
    edge_send,
    edge_recv,
):
    wide = lax.axis_index("wide")
    level = lax.axis_index("narrow")
    above = (wide, lax.rem(level + 1, DEPTH))
    below = (wide, lax.rem(level + DEPTH - 1, DEPTH))

    load = pltpu.make_async_copy(features, held, load_sem)
    load.start()
    barrier = pltpu.get_barrier_semaphore()
    for neighbour in (above, below):
        pl.semaphore_signal(barrier, inc=1, device_id=neighbour, device_id_type=MESH)
    pl.semaphore_wait(barrier, 2)

    running = running_counts(occupied)
    halos = functools.partial(halo_copies, tiles, halo_send, halo_recv, above, below)
    edges = functools.partial(
        edge_copies, low, high, from_upper, from_lower, edge_send, edge_recv, above, below
    )
    load.wait()

    @pl.loop(0, slots)
    def _(s):
        tiles[s, :, 16:80, :] = held[block_of_rank(running, s)]
        for copy in halos(s):
            copy.start()

    for planes in (acts_in, acts_mid):
        planes[0:TAPS, :] = jnp.zeros((TAPS, BX), bf16)
        planes[(TZ + 1) * TAPS : (TZ + 2) * TAPS, :] = jnp.zeros((TAPS, BX), bf16)
    build_banded(taps_one, mixed, w_one)
    build_banded(taps_two, mixed, w_two)
    build_head(w_head, w_top)

    work_through(
        slots,
        level,
        tiles,
        acts_in,
        acts_mid,
        w_one,
        w_two,
        w_top,
        result,
        low,
        high,
        finished,
        from_lower,
        from_upper,
        halos,
        edges,
        lambda s: None,
    )

    for b in range(BLK):
        kept = finished[running[b] - occupied[b]]
        out[b] = jnp.where(occupied[b] > 0, kept, jnp.zeros_like(kept))


SLOTS = 7
SURE = 3
GROUPS = ((0, 4, 3), (4, 8, 4), (8, 10, 5))
LANES = 10
TWINS = 4
TARGET = 5
COLUMNS = 32


def lane_step(lane, core):
    if lane < 8:
        sign = (1, -1, 1, -1)[lane - TWINS]
        return (sign, 0) if lane < TWINS + 2 else (0, sign)
    sign = (1, -1)[lane - 8]
    return sign * (1 - core), sign * core


def column_at(x, y, core):
    return (x % 4 * 4 + y % 4) * 2 + core


def lane_columns(lane, sign):
    column = lax.axis_index("wide")
    core, y, x = column % 2, column // 2 % 4, column // 8
    if lane < TWINS:
        return column_at(x, y, 1 - core)
    over_x, over_y = lane_step(lane, core)
    return column_at(x + sign * over_x + 4, y + sign * over_y + 4, core)


def turned(value, dim, step):
    step = step % 4
    if step == 0:
        return value
    head = lax.slice_in_dim(value, 0, step, axis=dim)
    return jnp.concatenate([lax.slice_in_dim(value, step, 4, axis=dim), head], axis=dim)


def across(value, kind, sign):
    if kind == 0:
        return jnp.concatenate([value[:, :, 1:2], value[:, :, 0:1]], axis=2)
    if kind < 5:
        over_x, over_y = lane_step(kind + TWINS - 1, 0)
        return turned(turned(value, 0, sign * over_x), 1, sign * over_y)
    step = sign * (1, -1)[kind - 5]
    over_x, over_y = turned(value, 0, step), turned(value, 1, step)
    return jnp.concatenate([over_x[:, :, 0:1], over_y[:, :, 1:2]], axis=2)


def make_plan(counts, used):
    load = counts
    own = counts
    kinds = 7
    for turn in range(2):
        for kind in range(kinds):
            gap = load - across(load, kind, 1)
            before = used[kind].reshape(load.shape) if turn > 0 else jnp.zeros_like(load)
            if kind == 0:
                sends = jnp.minimum(jnp.minimum(TWINS - before, own), gap >> 1)
                sends = jnp.maximum(jnp.minimum(sends, load - TARGET), 0)
            else:
                sends = (load > TARGET) & (gap >= 2) & (own > 0) & (before == 0)
                sends = jnp.where(sends, 1, 0)
            used[kind] = (before + sends).reshape(used.shape[1:])
            own = own - sends
            load = load - sends + across(sends, kind, -1)
    need = jnp.maximum(own, SURE)
    for kinds, start in (((0,), 3), ((1, 2, 3, 4), 4), ((5, 6), 5)):
        taken = jnp.zeros_like(load)
        for kind in kinds:
            taken = taken + across(used[kind].reshape(load.shape), kind, -1)
        need = jnp.where(taken > 0, jnp.maximum(need, start) + taken, need)
    used[7, 0] = jnp.max(need.reshape((COLUMNS,) + need.shape[3:]), axis=0)


def shared_kernel(
    occupied,
    features,
    taps_one,
    taps_two,
    w_head,
    out,
    needed,
    held,
    tiles,
    acts_in,
    acts_mid,
    w_one,
    w_two,
    w_top,
    mixed,
    result,
    low,
    high,
    from_upper,
    from_lower,
    finished,
    counts,
    used,
    out_a,
    out_b,
    out_c,
    in_a,
    in_b,
    in_c,
    back_out,
    back_in,
    load_sem,
    count_send,
    count_recv,
    lane_send,
    lane_recv,
    back_send,
    back_recv,
    halo_send,
    halo_recv,
    edge_send,
    edge_recv,
):
    wide = lax.axis_index("wide")
    level = lax.axis_index("narrow")
    above = (wide, lax.rem(level + 1, DEPTH))
    below = (wide, lax.rem(level + DEPTH - 1, DEPTH))

    core, y, x = wide % 2, wide // 2 % 4, wide // 8

    load = pltpu.make_async_copy(features, held, load_sem)
    load.start()
    peers = [
        [column_at(x, y, 1 - core)],
        [column_at(x, y + d, core) for d in (1, 2, 3)],
        [column_at(x + d, y, core) for d in (1, 2, 3)],
    ]
    barrier = pltpu.get_barrier_semaphore()
    greeted = [above, below] + [(column, level) for part in peers for column in part]
    for device in greeted:
        pl.semaphore_signal(barrier, inc=1, device_id=device, device_id_type=MESH)

    running = running_counts(occupied)
    held_blocks = running[-1]
    counts[x, y, core] = jnp.full((8, 128), held_blocks, jnp.int32)
    parts = [counts.at[x, y, core], counts.at[x, y], counts.at[x]]

    def count_copies(turn):
        copies = []
        for d, column in enumerate(peers[turn]):
            at = 3 * turn + d
            copies.append(
                pltpu.make_async_remote_copy(
                    src_ref=parts[turn],
                    dst_ref=parts[turn],
                    send_sem=count_send.at[at],
                    recv_sem=count_recv.at[at],
                    device_id=(column, level),
                    device_id_type=MESH,
                )
            )
        return copies

    outs, ins = (out_a, out_b, out_c), (in_a, in_b, in_c)

    def lane_copy(group, lane):
        at = lane - GROUPS[group][0]
        return pltpu.make_async_remote_copy(
            src_ref=outs[group].at[at],
            dst_ref=ins[group].at[at],
            send_sem=lane_send.at[lane],
            recv_sem=lane_recv.at[lane],
            device_id=(lane_columns(lane, 1), level),
            device_id_type=MESH,
        )

    def back_copy(lane):
        return pltpu.make_async_remote_copy(
            src_ref=back_out.at[lane],
            dst_ref=back_in.at[lane],
            send_sem=back_send.at[lane],
            recv_sem=back_recv.at[lane],
            device_id=(lane_columns(lane, -1), level),
            device_id_type=MESH,
        )

    halos = functools.partial(halo_copies, tiles, halo_send, halo_recv, above, below)
    edges = functools.partial(
        edge_copies, low, high, from_upper, from_lower, edge_send, edge_recv, above, below
    )

    build_banded(taps_one, mixed, w_one)
    for planes in (acts_in, acts_mid):
        planes[0:TAPS, :] = jnp.zeros((TAPS, BX), bf16)
        planes[(TZ + 1) * TAPS : (TZ + 2) * TAPS, :] = jnp.zeros((TAPS, BX), bf16)
    pl.semaphore_wait(barrier, len(greeted))
    for copy in count_copies(0):
        copy.start()
    load.wait()
    for s in range(SURE):
        tiles[s, :, 16:80, :] = held[block_of_rank(running, s)]
        for copy in halos(s):
            copy.start()
    for copy in count_copies(0):
        copy.wait()
    for copy in count_copies(1):
        copy.start()
    build_banded(taps_two, mixed, w_two)
    for copy in count_copies(1):
        copy.wait()
    for copy in count_copies(2):
        copy.start()
    build_head(w_head, w_top)
    for copy in count_copies(2):
        copy.wait()

    make_plan(counts[...], used)
    needed[0] = used[7, 0, 0, 0]
    sent, taken = [], []
    for lane in range(LANES):
        source = lane_columns(lane, -1)
        if lane < TWINS:
            sent.append(jnp.where(used[0, wide, 0, 0] > lane, 1, 0))
            taken.append(jnp.where(used[0, source, 0, 0] > lane, 1, 0))
        else:
            sent.append(used[lane - TWINS + 1, wide, 0, 0])
            taken.append(used[lane - TWINS + 1, source, 0, 0])
    kept = held_blocks - sum(sent)
    ranks = []
    rank = kept
    for lane in range(LANES):
        ranks.append(rank)
        rank = rank + sent[lane]
    places = []
    place = jnp.maximum(kept, SURE)
    for start, end, first in GROUPS:
        place = jnp.maximum(place, first)
        for lane in range(start, end):
            places.append(place)
            place = place + taken[lane]

    def send(group):
        start, end, _ = GROUPS[group]
        for lane in range(start, end):
            outs[group][lane - start] = held[block_of_rank(running, ranks[lane])]
            lane_copy(group, lane).start()

    def receive(group):
        for lane in range(*GROUPS[group][:2]):
            lane_copy(group, lane).wait()

    def stage(s):
        value = held[block_of_rank(running, s)]
        for group, (start, end, first) in enumerate(GROUPS):
            if s < first:
                continue
            chosen, found = jnp.int32(0), jnp.int32(0)
            for lane in range(start, end):
                here = (taken[lane] > 0) & (places[lane] == s)
                chosen = chosen + jnp.where(here, lane - start, 0)
                found = found + jnp.where(here, 1, 0)
            value = jnp.where(found > 0, ins[group][chosen], value)
        tiles[s, :, 16:80, :] = value
        for copy in halos(s):
            copy.start()

    send(0)
    send(1)

    def before(s):
        @pl.when(s == 2)
        def _():
            receive(0)
            stage(3)
            send(2)

        @pl.when(s == 3)
        def _():
            receive(1)
            stage(4)

        @pl.when(s == 4)
        def _():
            receive(2)
            stage(5)
            stage(6)

    work_through(
        SLOTS,
        level,
        tiles,
        acts_in,
        acts_mid,
        w_one,
        w_two,
        w_top,
        result,
        low,
        high,
        finished,
        from_lower,
        from_upper,
        halos,
        edges,
        before,
    )

    for lane in range(LANES):
        back_out[lane] = finished[jnp.clip(places[lane], 0, SLOTS - 1)]
        back_copy(lane).start()
    for lane in range(LANES):
        back_copy(lane).wait()

    for b in range(BLK):
        rank = running[b] - occupied[b]
        chosen = jnp.int32(0)
        for lane in range(LANES):
            chosen = chosen + jnp.where((sent[lane] > 0) & (ranks[lane] == rank), lane, 0)
        local = finished[jnp.minimum(rank, SLOTS - 1)]
        value = jnp.where(rank < kept, local, back_in[chosen])
        out[b] = jnp.where(occupied[b] > 0, value, jnp.zeros_like(value))


def work_scratch(slots):
    return [
        pltpu.VMEM((BLK, C, ZD * BY, BX), bf16),
        pltpu.VMEM((slots, C, TZ * BY, BX), bf16),
        pltpu.VMEM(((TZ + 2) * TAPS, BX), bf16),
        pltpu.VMEM(((TZ + 2) * TAPS, BX), bf16),
        pltpu.VMEM((ROWS, 9 * ROWS), bf16),
        pltpu.VMEM((ROWS, 9 * ROWS), bf16),
        pltpu.VMEM((AFF * BY, ROWS), bf16),
        pltpu.VMEM((ROWS, 9 * ROWS), bf16),
        pltpu.VMEM((slots, ZD, AFF * BY, BX), f32),
        pltpu.VMEM((slots, 2 * AFF * BY, BX), bf16),
        pltpu.VMEM((slots, 2 * AFF * BY, BX), bf16),
        pltpu.VMEM((slots, 2 * AFF * BY, BX), bf16),
        pltpu.VMEM((slots, 2 * AFF * BY, BX), bf16),
        pltpu.VMEM((slots, AFF, ZD * BY, BX), bf16),
    ]


def on_device(features, occupied, w_first, w_second, w_head):
    vmem = pl.BlockSpec(memory_space=pltpu.VMEM)
    in_specs = [
        pl.BlockSpec(memory_space=pltpu.SMEM),
        pl.BlockSpec(memory_space=pl.ANY),
        vmem,
        vmem,
        vmem,
    ]
    affinities = jax.ShapeDtypeStruct((BLK, AFF, ZD * BY, BX), bf16)
    dma = pltpu.SemaphoreType.DMA
    shared = pl.pallas_call(
        shared_kernel,
        out_shape=[affinities, jax.ShapeDtypeStruct((1,), jnp.int32)],
        in_specs=in_specs,
        out_specs=[vmem, pl.BlockSpec(memory_space=pltpu.SMEM)],
        scratch_shapes=work_scratch(SLOTS)
        + [
            pltpu.VMEM((4, 4, 2, 8, 128), jnp.int32),
            pltpu.VMEM((8, COLUMNS, 8, 128), jnp.int32),
        ]
        + [pltpu.VMEM((end - start, C, ZD * BY, BX), bf16) for start, end, _ in GROUPS * 2]
        + [
            pltpu.VMEM((LANES, AFF, ZD * BY, BX), bf16),
            pltpu.VMEM((LANES, AFF, ZD * BY, BX), bf16),
            dma,
            dma((9,)),
            dma((9,)),
            dma((LANES,)),
            dma((LANES,)),
            dma((LANES,)),
            dma((LANES,)),
            dma((SLOTS, 2)),
            dma((SLOTS, 2)),
            dma((SLOTS, 2)),
            dma((SLOTS, 2)),
        ],
        compiler_params=pltpu.CompilerParams(
            collective_id=0, has_side_effects=True, vmem_limit_bytes=56 << 20
        ),
    )
    whole = pl.pallas_call(
        functools.partial(whole_kernel, BLK),
        out_shape=affinities,
        in_specs=in_specs,
        out_specs=vmem,
        scratch_shapes=work_scratch(BLK)
        + [dma, dma((BLK, 2)), dma((BLK, 2)), dma((BLK, 2)), dma((BLK, 2))],
        compiler_params=pltpu.CompilerParams(
            collective_id=1, has_side_effects=True, vmem_limit_bytes=56 << 20
        ),
    )
    taps = [
        jnp.transpose(w, (2, 3, 4, 0, 1)).reshape(27 * C, C) for w in (w_first, w_second)
    ]
    args = (occupied, features.reshape(BLK, C, ZD * BY, BX), *taps, w_head)
    out, needed = shared(*args)
    out = lax.cond(needed[0] > SLOTS, lambda: whole(*args), lambda: out)
    return out.reshape(BLK, AFF, ZD, BY, BX)


def solution(mesh):
    in_specs = (P("wide", None, "narrow", None, None), P("wide"), P(), P(), P())
    out_specs = P("wide", None, "narrow", None, None)
    return jax.shard_map(
        on_device, mesh=mesh, in_specs=in_specs, out_specs=out_specs, check_vma=False
    )
```

```python
import functools

import jax
import jax.numpy as jnp
from jax import lax
from jax.experimental import pallas as pl
from jax.experimental.pallas import tpu as pltpu
from jax.sharding import PartitionSpec as P

C = 32
AFF = 3
BLK = 16
BY = 8
BX = 128
ZD = 8
TZ = 12
ROWS = C * BY
TAPS = 3 * ROWS
BLEND = tuple(min(1.0, (t + 0.5) / 4, (TZ - t - 0.5) / 4) for t in range(TZ))
MESH = pl.DeviceIdType.MESH
f32 = jnp.float32
bf16 = jnp.bfloat16


def iota(shape, dim):
    return lax.broadcasted_iota(jnp.int32, shape, dim)


def put_shifted(planes, z, value, first, last):
    base = (z + 1) * TAPS
    value = value.astype(bf16)
    nothing = jnp.zeros_like(value)
    planes[base : base + ROWS, :] = jnp.where(first, nothing, pltpu.roll(value, 1, 1))
    planes[base + ROWS : base + 2 * ROWS, :] = value
    planes[base + 2 * ROWS : base + TAPS, :] = jnp.where(
        last, nothing, pltpu.roll(value, BX - 1, 1)
    )


def conv_pair(planes, weight, pair):
    base = 2 * pair * TAPS
    gathered = jnp.concatenate(
        [planes[base : base + 3 * TAPS, :], planes[base + TAPS : base + 4 * TAPS, :]], axis=1
    )
    return jnp.dot(weight[...], gathered, preferred_element_type=f32)


def work_through(
    slots,
    level,
    tiles,
    acts_in,
    acts_mid,
    w_one,
    w_two,
    w_top,
    result,
    low,
    high,
    finished,
    from_lower,
    from_upper,
    halos,
    edges,
    before,
):
    lane = iota((ROWS, BX), 1)
    first, last = lane == 0, lane == BX - 1

    def prepare(s, p):
        value = tiles[s, :, 16 * p : 16 * p + 16, :].astype(f32)
        if p == 0:
            value = jnp.where(level > 0, value, 0.0)
        if p == 5:
            value = jnp.where(level < DEPTH - 1, value, 0.0)
        value = value.reshape(C, 2, BY, BX)
        put_shifted(acts_in, 2 * p, value[:, 0].reshape(ROWS, BX), first, last)
        put_shifted(acts_in, 2 * p + 1, value[:, 1].reshape(ROWS, BX), first, last)

    def conv_one(p):
        value = jnp.maximum(conv_pair(acts_in, w_one, p), 0.0)
        put_shifted(acts_mid, 2 * p, value[:, :BX], first, last)
        put_shifted(acts_mid, 2 * p + 1, value[:, BX:], first, last)

    def conv_two(p):
        base = (2 * p + 1) * TAPS + ROWS
        own = jnp.concatenate(
            [acts_in[base : base + ROWS, :], acts_in[base + TAPS : base + TAPS + ROWS, :]], axis=1
        )
        value = conv_pair(acts_mid, w_two, p) + own.astype(f32)
        return jnp.maximum(value, 0.0).astype(bf16)

    def head(s, p, acts):
        value = jnp.dot(w_top[...], acts, preferred_element_type=f32)
        pair = [value[:, :BX] * BLEND[2 * p], value[:, BX:] * BLEND[2 * p + 1]]
        if p == 0:
            low[s] = jnp.concatenate(pair, axis=0).astype(bf16)
        elif p == 5:
            high[s] = jnp.concatenate(pair, axis=0).astype(bf16)
        else:
            result[s, 2 * p - 2] = pair[0]
            result[s, 2 * p - 1] = pair[1]

    def close(s):
        for copy in edges(s):
            copy.wait()
        finish(result, from_lower, from_upper, finished, s, level)

    @pl.loop(0, slots)
    def _(s):
        before(s)

        @pl.when(s > 1)
        def _():
            for copy in edges(s - 2):
                copy.start()

        @pl.when(s > 2)
        def _():
            close(s - 3)

        for copy in halos(s):
            copy.wait()
        previous = jnp.maximum(s - 1, 0)
        acts_4 = conv_two(4)
        prepare(s, 0)
        prepare(s, 1)
        acts_5 = conv_two(5)
        conv_one(0)
        prepare(s, 2)
        head(previous, 4, acts_4)
        conv_one(1)
        prepare(s, 3)
        head(previous, 5, acts_5)
        conv_one(2)
        prepare(s, 4)
        acts_0 = conv_two(0)
        conv_one(3)
        prepare(s, 5)
        acts_1 = conv_two(1)
        head(s, 0, acts_0)
        conv_one(4)
        acts_2 = conv_two(2)
        head(s, 1, acts_1)
        conv_one(5)
        acts_3 = conv_two(3)
        head(s, 2, acts_2)
        head(s, 3, acts_3)

    for copy in edges(slots - 2):
        copy.start()
    acts_4 = conv_two(4)
    acts_5 = conv_two(5)
    head(slots - 1, 4, acts_4)
    head(slots - 1, 5, acts_5)
    for copy in edges(slots - 1):
        copy.start()
    for s in range(slots - 3, slots):
        close(s)


def build_banded(taps, mixed, banded):
    blocks = []
    for outer in range(9):
        rows = [((outer // 3 * 3 + dy) * 3 + outer % 3) * C for dy in range(3)]
        blocks.append(
            jnp.concatenate([taps[at : at + C, :].astype(f32) for at in rows], axis=1)
        )
    stacked = jnp.concatenate(blocks, axis=0).astype(bf16)
    row, col = iota((3 * C, ROWS), 0), iota((3 * C, ROWS), 1)
    same = row % C == col // BY
    for y in range(BY):
        spread = (same & (col % BY == y + row // C - 1)).astype(bf16)
        wide = jnp.dot(stacked, spread, preferred_element_type=f32).astype(bf16)
        for outer in range(9):
            mixed[y * C : (y + 1) * C, outer * ROWS : (outer + 1) * ROWS] = wide[
                outer * C : (outer + 1) * C
            ]
    row, col = iota((ROWS, ROWS), 0), iota((ROWS, ROWS), 1)
    order = ((row // BY == col % C) & (row % BY == col // C)).astype(bf16)
    for outer in range(9):
        cut = slice(outer * ROWS, (outer + 1) * ROWS)
        banded[:, cut] = jnp.dot(order, mixed[:, cut], preferred_element_type=f32).astype(bf16)


def build_head(w_head, banded):
    spread = (iota((C, ROWS), 1) // BY == iota((C, ROWS), 0)).astype(bf16)
    wide = jnp.dot(w_head[...], spread, preferred_element_type=f32)
    wide = jnp.broadcast_to(wide[:, None, :], (AFF, BY, ROWS)).reshape(AFF * BY, ROWS)
    apart = iota((AFF * BY, ROWS), 1) % BY - iota((AFF * BY, ROWS), 0) % BY
    banded[...] = jnp.where(apart == 0, wide, 0.0).astype(bf16)


DEPTH = 4


def running_counts(occupied):
    running = []
    count = jnp.int32(0)
    for b in range(BLK):
        count = count + occupied[b]
        running.append(count)
    return running


def block_of_rank(running, rank):
    picked = jnp.int32(0)
    for b in range(BLK):
        picked = picked + jnp.where(running[b] <= rank, 1, 0)
    return jnp.minimum(picked, BLK - 1)


def halo_copies(tiles, send, recv, above, below, s):
    down = pltpu.make_async_remote_copy(
        src_ref=tiles.at[s, :, 16:32, :],
        dst_ref=tiles.at[s, :, 80:96, :],
        send_sem=send.at[s, 0],
        recv_sem=recv.at[s, 0],
        device_id=below,
        device_id_type=MESH,
    )
    up = pltpu.make_async_remote_copy(
        src_ref=tiles.at[s, :, 64:80, :],
        dst_ref=tiles.at[s, :, 0:16, :],
        send_sem=send.at[s, 1],
        recv_sem=recv.at[s, 1],
        device_id=above,
        device_id_type=MESH,
    )
    return down, up


def edge_copies(low, high, from_upper, from_lower, send, recv, above, below, s):
    down = pltpu.make_async_remote_copy(
        src_ref=low.at[s],
        dst_ref=from_upper.at[s],
        send_sem=send.at[s, 0],
        recv_sem=recv.at[s, 0],
        device_id=below,
        device_id_type=MESH,
    )
    up = pltpu.make_async_remote_copy(
        src_ref=high.at[s],
        dst_ref=from_lower.at[s],
        send_sem=send.at[s, 1],
        recv_sem=recv.at[s, 1],
        device_id=above,
        device_id_type=MESH,
    )
    return down, up


def finish(result, from_lower, from_upper, finished, s, level):
    has_lower, has_upper = level > 0, level < DEPTH - 1
    planes = [result[s, z] for z in range(ZD)]
    lower = from_lower[s].astype(f32)
    upper = from_upper[s].astype(f32)
    for i in range(2):
        part = lower[24 * i : 24 * i + 24]
        planes[i] = jnp.where(has_lower, planes[i] + part, planes[i] / BLEND[2 + i])
        part = upper[24 * i : 24 * i + 24]
        planes[6 + i] = jnp.where(has_upper, planes[6 + i] + part, planes[6 + i] / BLEND[8 + i])
    for a in range(AFF):
        for p in range(4):
            two = [planes[2 * p + i][BY * a : BY * a + BY] for i in range(2)]
            finished[s, a, 16 * p : 16 * p + 16, :] = jnp.concatenate(two, axis=0).astype(bf16)


def whole_kernel(
    slots,
    occupied,
    features,
    taps_one,
    taps_two,
    w_head,
    out,
    held,
    tiles,
    acts_in,
    acts_mid,
    w_one,
    w_two,
    w_top,
    mixed,
    result,
    low,
    high,
    from_upper,
    from_lower,
    finished,
    load_sem,
    halo_send,
    halo_recv,
    edge_send,
    edge_recv,
):
    wide = lax.axis_index("wide")
    level = lax.axis_index("narrow")
    above = (wide, lax.rem(level + 1, DEPTH))
    below = (wide, lax.rem(level + DEPTH - 1, DEPTH))

    load = pltpu.make_async_copy(features, held, load_sem)
    load.start()
    barrier = pltpu.get_barrier_semaphore()
    for neighbour in (above, below):
        pl.semaphore_signal(barrier, inc=1, device_id=neighbour, device_id_type=MESH)
    pl.semaphore_wait(barrier, 2)

    running = running_counts(occupied)
    halos = functools.partial(halo_copies, tiles, halo_send, halo_recv, above, below)
    edges = functools.partial(
        edge_copies, low, high, from_upper, from_lower, edge_send, edge_recv, above, below
    )
    load.wait()

    @pl.loop(0, slots)
    def _(s):
        tiles[s, :, 16:80, :] = held[block_of_rank(running, s)]
        for copy in halos(s):
            copy.start()

    for planes in (acts_in, acts_mid):
        planes[0:TAPS, :] = jnp.zeros((TAPS, BX), bf16)
        planes[(TZ + 1) * TAPS : (TZ + 2) * TAPS, :] = jnp.zeros((TAPS, BX), bf16)
    build_banded(taps_one, mixed, w_one)
    build_banded(taps_two, mixed, w_two)
    build_head(w_head, w_top)

    work_through(
        slots,
        level,
        tiles,
        acts_in,
        acts_mid,
        w_one,
        w_two,
        w_top,
        result,
        low,
        high,
        finished,
        from_lower,
        from_upper,
        halos,
        edges,
        lambda s: None,
    )

    for b in range(BLK):
        kept = finished[running[b] - occupied[b]]
        out[b] = jnp.where(occupied[b] > 0, kept, jnp.zeros_like(kept))


SLOTS = 7
SURE = 3
GROUPS = ((0, 4, 3), (4, 8, 4), (8, 10, 5))
LANES = 10
TWINS = 4
TARGET = 5
COLUMNS = 32


def lane_step(lane, core):
    if lane < 8:
        sign = (1, -1, 1, -1)[lane - TWINS]
        return (sign, 0) if lane < TWINS + 2 else (0, sign)
    sign = (1, -1)[lane - 8]
    return sign * (1 - core), sign * core


def column_at(x, y, core):
    return (x % 4 * 4 + y % 4) * 2 + core


def lane_columns(lane, sign):
    column = lax.axis_index("wide")
    core, y, x = column % 2, column // 2 % 4, column // 8
    if lane < TWINS:
        return column_at(x, y, 1 - core)
    over_x, over_y = lane_step(lane, core)
    return column_at(x + sign * over_x + 4, y + sign * over_y + 4, core)


def turned(value, dim, step):
    step = step % 4
    if step == 0:
        return value
    head = lax.slice_in_dim(value, 0, step, axis=dim)
    return jnp.concatenate([lax.slice_in_dim(value, step, 4, axis=dim), head], axis=dim)


def across(value, kind, sign):
    if kind == 0:
        return jnp.concatenate([value[:, :, 1:2], value[:, :, 0:1]], axis=2)
    if kind < 5:
        over_x, over_y = lane_step(kind + TWINS - 1, 0)
        return turned(turned(value, 0, sign * over_x), 1, sign * over_y)
    step = sign * (1, -1)[kind - 5]
    over_x, over_y = turned(value, 0, step), turned(value, 1, step)
    return jnp.concatenate([over_x[:, :, 0:1], over_y[:, :, 1:2]], axis=2)


def make_plan(counts, used):
    load = counts
    own = counts
    kinds = 7
    for turn in range(2):
        for kind in range(kinds):
            gap = load - across(load, kind, 1)
            before = used[kind].reshape(load.shape) if turn > 0 else jnp.zeros_like(load)
            if kind == 0:
                sends = jnp.minimum(jnp.minimum(TWINS - before, own), gap >> 1)
                sends = jnp.maximum(jnp.minimum(sends, load - TARGET), 0)
            else:
                sends = (load > TARGET) & (gap >= 2) & (own > 0) & (before == 0)
                sends = jnp.where(sends, 1, 0)
            used[kind] = (before + sends).reshape(used.shape[1:])
            own = own - sends
            load = load - sends + across(sends, kind, -1)
    need = jnp.maximum(own, SURE)
    for kinds, start in (((0,), 3), ((1, 2, 3, 4), 4), ((5, 6), 5)):
        taken = jnp.zeros_like(load)
        for kind in kinds:
            taken = taken + across(used[kind].reshape(load.shape), kind, -1)
        need = jnp.where(taken > 0, jnp.maximum(need, start) + taken, need)
    used[7, 0] = jnp.max(need.reshape((COLUMNS,) + need.shape[3:]), axis=0)


def shared_kernel(
    occupied,
    features,
    taps_one,
    taps_two,
    w_head,
    out,
    needed,
    held,
    tiles,
    acts_in,
    acts_mid,
    w_one,
    w_two,
    w_top,
    mixed,
    result,
    low,
    high,
    from_upper,
    from_lower,
    finished,
    counts,
    used,
    out_a,
    out_b,
    out_c,
    in_a,
    in_b,
    in_c,
    back_out,
    back_in,
    load_sem,
    count_send,
    count_recv,
    lane_send,
    lane_recv,
    back_send,
    back_recv,
    halo_send,
    halo_recv,
    edge_send,
    edge_recv,
):
    wide = lax.axis_index("wide")
    level = lax.axis_index("narrow")
    above = (wide, lax.rem(level + 1, DEPTH))
    below = (wide, lax.rem(level + DEPTH - 1, DEPTH))

    core, y, x = wide % 2, wide // 2 % 4, wide // 8

    load = pltpu.make_async_copy(features, held, load_sem)
    load.start()
    peers = [
        [column_at(x, y, 1 - core)],
        [column_at(x, y + d, core) for d in (1, 2, 3)],
        [column_at(x + d, y, core) for d in (1, 2, 3)],
    ]
    barrier = pltpu.get_barrier_semaphore()
    greeted = [above, below] + [(column, level) for part in peers for column in part]
    for device in greeted:
        pl.semaphore_signal(barrier, inc=1, device_id=device, device_id_type=MESH)

    running = running_counts(occupied)
    held_blocks = running[-1]
    counts[x, y, core] = jnp.full((8, 128), held_blocks, jnp.int32)
    parts = [counts.at[x, y, core], counts.at[x, y], counts.at[x]]

    def count_copies(turn):
        copies = []
        for d, column in enumerate(peers[turn]):
            at = 3 * turn + d
            copies.append(
                pltpu.make_async_remote_copy(
                    src_ref=parts[turn],
                    dst_ref=parts[turn],
                    send_sem=count_send.at[at],
                    recv_sem=count_recv.at[at],
                    device_id=(column, level),
                    device_id_type=MESH,
                )
            )
        return copies

    outs, ins = (out_a, out_b, out_c), (in_a, in_b, in_c)

    def lane_copy(group, lane):
        at = lane - GROUPS[group][0]
        return pltpu.make_async_remote_copy(
            src_ref=outs[group].at[at],
            dst_ref=ins[group].at[at],
            send_sem=lane_send.at[lane],
            recv_sem=lane_recv.at[lane],
            device_id=(lane_columns(lane, 1), level),
            device_id_type=MESH,
        )

    def back_copy(lane):
        return pltpu.make_async_remote_copy(
            src_ref=back_out.at[lane],
            dst_ref=back_in.at[lane],
            send_sem=back_send.at[lane],
            recv_sem=back_recv.at[lane],
            device_id=(lane_columns(lane, -1), level),
            device_id_type=MESH,
        )

    halos = functools.partial(halo_copies, tiles, halo_send, halo_recv, above, below)
    edges = functools.partial(
        edge_copies, low, high, from_upper, from_lower, edge_send, edge_recv, above, below
    )

    pl.semaphore_wait(barrier, len(greeted))
    for copy in count_copies(0):
        copy.start()
    build_banded(taps_one, mixed, w_one)
    for copy in count_copies(0):
        copy.wait()
    for copy in count_copies(1):
        copy.start()
    build_banded(taps_two, mixed, w_two)
    for copy in count_copies(1):
        copy.wait()
    for copy in count_copies(2):
        copy.start()
    load.wait()

    def stage_own(s):
        tiles[s, :, 16:80, :] = held[block_of_rank(running, s)]
        for copy in halos(s):
            copy.start()

    stage_own(0)
    build_head(w_head, w_top)
    for planes in (acts_in, acts_mid):
        planes[0:TAPS, :] = jnp.zeros((TAPS, BX), bf16)
        planes[(TZ + 1) * TAPS : (TZ + 2) * TAPS, :] = jnp.zeros((TAPS, BX), bf16)
    for copy in count_copies(2):
        copy.wait()
    make_plan(counts[...], used)
    needed[0] = used[7, 0, 0, 0]

    def schedule():
        sent, taken = [], []
        for lane in range(LANES):
            source = lane_columns(lane, -1)
            if lane < TWINS:
                sent.append(jnp.where(used[0, wide, 0, 0] > lane, 1, 0))
                taken.append(jnp.where(used[0, source, 0, 0] > lane, 1, 0))
            else:
                sent.append(used[lane - TWINS + 1, wide, 0, 0])
                taken.append(used[lane - TWINS + 1, source, 0, 0])
        kept = held_blocks - sum(sent)
        ranks = []
        rank = kept
        for lane in range(LANES):
            ranks.append(rank)
            rank = rank + sent[lane]
        places = []
        place = jnp.maximum(kept, SURE)
        for start, end, first in GROUPS:
            place = jnp.maximum(place, first)
            for lane in range(start, end):
                places.append(place)
                place = place + taken[lane]
        return kept, sent, ranks, taken, places

    def send(group):
        ranks = schedule()[2]
        start, end, _ = GROUPS[group]
        for lane in range(start, end):
            outs[group][lane - start] = held[block_of_rank(running, ranks[lane])]
            lane_copy(group, lane).start()

    def receive(group):
        for lane in range(*GROUPS[group][:2]):
            lane_copy(group, lane).wait()

    def stage(s):
        _, _, _, taken, places = schedule()
        value = held[block_of_rank(running, s)]
        for group, (start, end, first) in enumerate(GROUPS):
            if s < first:
                continue
            chosen, found = jnp.int32(0), jnp.int32(0)
            for lane in range(start, end):
                here = (taken[lane] > 0) & (places[lane] == s)
                chosen = chosen + jnp.where(here, lane - start, 0)
                found = found + jnp.where(here, 1, 0)
            value = jnp.where(found > 0, ins[group][chosen], value)
        tiles[s, :, 16:80, :] = value
        for copy in halos(s):
            copy.start()

    def before(s):
        @pl.when(s < SURE - 1)
        def _():
            stage_own(s + 1)

        @pl.when(s == 2)
        def _():
            receive(0)
            stage(3)
            send(2)

        @pl.when(s == 3)
        def _():
            receive(1)
            stage(4)

        @pl.when(s == 4)
        def _():
            receive(2)
            stage(5)

        @pl.when(s == 5)
        def _():
            stage(6)

    send(1)
    send(0)
    work_through(
        SLOTS,
        level,
        tiles,
        acts_in,
        acts_mid,
        w_one,
        w_two,
        w_top,
        result,
        low,
        high,
        finished,
        from_lower,
        from_upper,
        halos,
        edges,
        before,
    )

    kept, sent, ranks, _, places = schedule()
    for lane in reversed(range(LANES)):
        back_out[lane] = finished[jnp.clip(places[lane], 0, SLOTS - 1)]
        back_copy(lane).start()
    for lane in range(LANES):
        back_copy(lane).wait()

    for b in range(BLK):
        rank = running[b] - occupied[b]
        chosen = jnp.int32(0)
        for lane in range(LANES):
            chosen = chosen + jnp.where((sent[lane] > 0) & (ranks[lane] == rank), lane, 0)
        local = finished[jnp.minimum(rank, SLOTS - 1)]
        value = jnp.where(rank < kept, local, back_in[chosen])
        out[b] = jnp.where(occupied[b] > 0, value, jnp.zeros_like(value))


def work_scratch(slots):
    return [
        pltpu.VMEM((BLK, C, ZD * BY, BX), bf16),
        pltpu.VMEM((slots, C, TZ * BY, BX), bf16),
        pltpu.VMEM(((TZ + 2) * TAPS, BX), bf16),
        pltpu.VMEM(((TZ + 2) * TAPS, BX), bf16),
        pltpu.VMEM((ROWS, 9 * ROWS), bf16),
        pltpu.VMEM((ROWS, 9 * ROWS), bf16),
        pltpu.VMEM((AFF * BY, ROWS), bf16),
        pltpu.VMEM((ROWS, 9 * ROWS), bf16),
        pltpu.VMEM((slots, ZD, AFF * BY, BX), f32),
        pltpu.VMEM((slots, 2 * AFF * BY, BX), bf16),
        pltpu.VMEM((slots, 2 * AFF * BY, BX), bf16),
        pltpu.VMEM((slots, 2 * AFF * BY, BX), bf16),
        pltpu.VMEM((slots, 2 * AFF * BY, BX), bf16),
        pltpu.VMEM((slots, AFF, ZD * BY, BX), bf16),
    ]


def on_device(features, occupied, w_first, w_second, w_head):
    vmem = pl.BlockSpec(memory_space=pltpu.VMEM)
    in_specs = [
        pl.BlockSpec(memory_space=pltpu.SMEM),
        pl.BlockSpec(memory_space=pl.ANY),
        vmem,
        vmem,
        vmem,
    ]
    affinities = jax.ShapeDtypeStruct((BLK, AFF, ZD * BY, BX), bf16)
    dma = pltpu.SemaphoreType.DMA
    shared = pl.pallas_call(
        shared_kernel,
        out_shape=[affinities, jax.ShapeDtypeStruct((1,), jnp.int32)],
        in_specs=in_specs,
        out_specs=[vmem, pl.BlockSpec(memory_space=pltpu.SMEM)],
        scratch_shapes=work_scratch(SLOTS)
        + [
            pltpu.VMEM((4, 4, 2, 8, 128), jnp.int32),
            pltpu.VMEM((8, COLUMNS, 8, 128), jnp.int32),
        ]
        + [pltpu.VMEM((end - start, C, ZD * BY, BX), bf16) for start, end, _ in GROUPS * 2]
        + [
            pltpu.VMEM((LANES, AFF, ZD * BY, BX), bf16),
            pltpu.VMEM((LANES, AFF, ZD * BY, BX), bf16),
            dma,
            dma((9,)),
            dma((9,)),
            dma((LANES,)),
            dma((LANES,)),
            dma((LANES,)),
            dma((LANES,)),
            dma((SLOTS, 2)),
            dma((SLOTS, 2)),
            dma((SLOTS, 2)),
            dma((SLOTS, 2)),
        ],
        compiler_params=pltpu.CompilerParams(
            collective_id=0, has_side_effects=True, vmem_limit_bytes=56 << 20
        ),
    )
    whole = pl.pallas_call(
        functools.partial(whole_kernel, BLK),
        out_shape=affinities,
        in_specs=in_specs,
        out_specs=vmem,
        scratch_shapes=work_scratch(BLK)
        + [dma, dma((BLK, 2)), dma((BLK, 2)), dma((BLK, 2)), dma((BLK, 2))],
        compiler_params=pltpu.CompilerParams(
            collective_id=1, has_side_effects=True, vmem_limit_bytes=56 << 20
        ),
    )
    taps = [
        jnp.transpose(w, (2, 3, 4, 0, 1)).reshape(27 * C, C) for w in (w_first, w_second)
    ]
    args = (occupied, features.reshape(BLK, C, ZD * BY, BX), *taps, w_head)
    out, needed = shared(*args)
    out = lax.cond(needed[0] > SLOTS, lambda: whole(*args), lambda: out)
    return out.reshape(BLK, AFF, ZD, BY, BX)


def solution(mesh):
    in_specs = (P("wide", None, "narrow", None, None), P("wide"), P(), P(), P())
    out_specs = P("wide", None, "narrow", None, None)
    return jax.shard_map(
        on_device, mesh=mesh, in_specs=in_specs, out_specs=out_specs, check_vma=False
    )
```

```python
import functools

import jax
import jax.numpy as jnp
from jax import lax
from jax.experimental import pallas as pl
from jax.experimental.pallas import tpu as pltpu
from jax.sharding import PartitionSpec as P

C = 32
AFF = 3
BLK = 16
BY = 8
BX = 128
ZD = 8
TZ = 12
ROWS = C * BY
TAPS = 3 * ROWS
BLEND = tuple(min(1.0, (t + 0.5) / 4, (TZ - t - 0.5) / 4) for t in range(TZ))
MESH = pl.DeviceIdType.MESH
f32 = jnp.float32
bf16 = jnp.bfloat16


def iota(shape, dim):
    return lax.broadcasted_iota(jnp.int32, shape, dim)


def put_shifted(planes, z, value, first, last):
    base = (z + 1) * TAPS
    value = value.astype(bf16)
    nothing = jnp.zeros_like(value)
    planes[base : base + ROWS, :] = jnp.where(first, nothing, pltpu.roll(value, 1, 1))
    planes[base + ROWS : base + 2 * ROWS, :] = value
    planes[base + 2 * ROWS : base + TAPS, :] = jnp.where(
        last, nothing, pltpu.roll(value, BX - 1, 1)
    )


def conv_pair(planes, weight, pair):
    base = 2 * pair * TAPS
    gathered = jnp.concatenate(
        [planes[base : base + 3 * TAPS, :], planes[base + TAPS : base + 4 * TAPS, :]], axis=1
    )
    return jnp.dot(weight[...], gathered, preferred_element_type=f32)


def work_through(
    slots,
    level,
    tiles,
    acts_in,
    acts_mid,
    w_one,
    w_two,
    w_top,
    result,
    low,
    high,
    finished,
    from_lower,
    from_upper,
    halos,
    edges,
    before,
):
    lane = iota((ROWS, BX), 1)
    first, last = lane == 0, lane == BX - 1

    def prepare(s, p):
        value = tiles[s, :, 16 * p : 16 * p + 16, :].astype(f32)
        if p == 0:
            value = jnp.where(level > 0, value, 0.0)
        if p == 5:
            value = jnp.where(level < DEPTH - 1, value, 0.0)
        value = value.reshape(C, 2, BY, BX)
        put_shifted(acts_in, 2 * p, value[:, 0].reshape(ROWS, BX), first, last)
        put_shifted(acts_in, 2 * p + 1, value[:, 1].reshape(ROWS, BX), first, last)

    def conv_one(p):
        value = jnp.maximum(conv_pair(acts_in, w_one, p), 0.0)
        put_shifted(acts_mid, 2 * p, value[:, :BX], first, last)
        put_shifted(acts_mid, 2 * p + 1, value[:, BX:], first, last)

    def conv_two(p):
        base = (2 * p + 1) * TAPS + ROWS
        own = jnp.concatenate(
            [acts_in[base : base + ROWS, :], acts_in[base + TAPS : base + TAPS + ROWS, :]], axis=1
        )
        value = conv_pair(acts_mid, w_two, p) + own.astype(f32)
        return jnp.maximum(value, 0.0).astype(bf16)

    def head(s, p, acts):
        value = jnp.dot(w_top[...], acts, preferred_element_type=f32)
        pair = [value[:, :BX] * BLEND[2 * p], value[:, BX:] * BLEND[2 * p + 1]]
        if p == 0:
            low[s] = jnp.concatenate(pair, axis=0).astype(bf16)
        elif p == 5:
            high[s] = jnp.concatenate(pair, axis=0).astype(bf16)
        else:
            result[s, 2 * p - 2] = pair[0]
            result[s, 2 * p - 1] = pair[1]

    def close(s):
        for copy in edges(s):
            copy.wait()
        finish(result, from_lower, from_upper, finished, s, level)

    @pl.loop(0, slots)
    def _(s):
        before(s)

        @pl.when(s > 1)
        def _():
            for copy in edges(s - 2):
                copy.start()

        @pl.when(s > 2)
        def _():
            close(s - 3)

        for copy in halos(s):
            copy.wait()
        previous = jnp.maximum(s - 1, 0)
        acts_4 = conv_two(4)
        prepare(s, 0)
        prepare(s, 1)
        acts_5 = conv_two(5)
        conv_one(0)
        prepare(s, 2)
        head(previous, 4, acts_4)
        conv_one(1)
        prepare(s, 3)
        head(previous, 5, acts_5)
        conv_one(2)
        prepare(s, 4)
        acts_0 = conv_two(0)
        conv_one(3)
        prepare(s, 5)
        acts_1 = conv_two(1)
        head(s, 0, acts_0)
        conv_one(4)
        acts_2 = conv_two(2)
        head(s, 1, acts_1)
        conv_one(5)
        acts_3 = conv_two(3)
        head(s, 2, acts_2)
        head(s, 3, acts_3)

    for copy in edges(slots - 2):
        copy.start()
    acts_4 = conv_two(4)
    acts_5 = conv_two(5)
    head(slots - 1, 4, acts_4)
    head(slots - 1, 5, acts_5)
    for copy in edges(slots - 1):
        copy.start()
    for s in range(slots - 3, slots):
        close(s)


def build_banded(taps, mixed, banded):
    blocks = []
    for outer in range(9):
        rows = [((outer // 3 * 3 + dy) * 3 + outer % 3) * C for dy in range(3)]
        blocks.append(
            jnp.concatenate([taps[at : at + C, :].astype(f32) for at in rows], axis=1)
        )
    stacked = jnp.concatenate(blocks, axis=0).astype(bf16)
    row, col = iota((3 * C, ROWS), 0), iota((3 * C, ROWS), 1)
    same = row % C == col // BY
    for y in range(BY):
        spread = (same & (col % BY == y + row // C - 1)).astype(bf16)
        wide = jnp.dot(stacked, spread, preferred_element_type=f32).astype(bf16)
        for outer in range(9):
            mixed[y * C : (y + 1) * C, outer * ROWS : (outer + 1) * ROWS] = wide[
                outer * C : (outer + 1) * C
            ]
    row, col = iota((ROWS, ROWS), 0), iota((ROWS, ROWS), 1)
    order = ((row // BY == col % C) & (row % BY == col // C)).astype(bf16)
    for outer in range(9):
        cut = slice(outer * ROWS, (outer + 1) * ROWS)
        banded[:, cut] = jnp.dot(order, mixed[:, cut], preferred_element_type=f32).astype(bf16)


def build_head(w_head, banded):
    spread = (iota((C, ROWS), 1) // BY == iota((C, ROWS), 0)).astype(bf16)
    wide = jnp.dot(w_head[...], spread, preferred_element_type=f32)
    wide = jnp.broadcast_to(wide[:, None, :], (AFF, BY, ROWS)).reshape(AFF * BY, ROWS)
    apart = iota((AFF * BY, ROWS), 1) % BY - iota((AFF * BY, ROWS), 0) % BY
    banded[...] = jnp.where(apart == 0, wide, 0.0).astype(bf16)


DEPTH = 4


def running_counts(occupied):
    running = []
    count = jnp.int32(0)
    for b in range(BLK):
        count = count + occupied[b]
        running.append(count)
    return running


def block_of_rank(running, rank):
    picked = jnp.int32(0)
    for b in range(BLK):
        picked = picked + jnp.where(running[b] <= rank, 1, 0)
    return jnp.minimum(picked, BLK - 1)


def halo_copies(tiles, send, recv, above, below, s):
    down = pltpu.make_async_remote_copy(
        src_ref=tiles.at[s, :, 16:32, :],
        dst_ref=tiles.at[s, :, 80:96, :],
        send_sem=send.at[s, 0],
        recv_sem=recv.at[s, 0],
        device_id=below,
        device_id_type=MESH,
    )
    up = pltpu.make_async_remote_copy(
        src_ref=tiles.at[s, :, 64:80, :],
        dst_ref=tiles.at[s, :, 0:16, :],
        send_sem=send.at[s, 1],
        recv_sem=recv.at[s, 1],
        device_id=above,
        device_id_type=MESH,
    )
    return down, up


def edge_copies(low, high, from_upper, from_lower, send, recv, above, below, s):
    down = pltpu.make_async_remote_copy(
        src_ref=low.at[s],
        dst_ref=from_upper.at[s],
        send_sem=send.at[s, 0],
        recv_sem=recv.at[s, 0],
        device_id=below,
        device_id_type=MESH,
    )
    up = pltpu.make_async_remote_copy(
        src_ref=high.at[s],
        dst_ref=from_lower.at[s],
        send_sem=send.at[s, 1],
        recv_sem=recv.at[s, 1],
        device_id=above,
        device_id_type=MESH,
    )
    return down, up


def finish(result, from_lower, from_upper, finished, s, level):
    has_lower, has_upper = level > 0, level < DEPTH - 1
    planes = [result[s, z] for z in range(ZD)]
    lower = from_lower[s].astype(f32)
    upper = from_upper[s].astype(f32)
    for i in range(2):
        part = lower[24 * i : 24 * i + 24]
        planes[i] = jnp.where(has_lower, planes[i] + part, planes[i] / BLEND[2 + i])
        part = upper[24 * i : 24 * i + 24]
        planes[6 + i] = jnp.where(has_upper, planes[6 + i] + part, planes[6 + i] / BLEND[8 + i])
    for a in range(AFF):
        for p in range(4):
            two = [planes[2 * p + i][BY * a : BY * a + BY] for i in range(2)]
            finished[s, a, 16 * p : 16 * p + 16, :] = jnp.concatenate(two, axis=0).astype(bf16)


def whole_kernel(
    slots,
    occupied,
    features,
    taps_one,
    taps_two,
    w_head,
    out,
    held,
    tiles,
    acts_in,
    acts_mid,
    w_one,
    w_two,
    w_top,
    mixed,
    result,
    low,
    high,
    from_upper,
    from_lower,
    finished,
    load_sem,
    halo_send,
    halo_recv,
    edge_send,
    edge_recv,
):
    wide = lax.axis_index("wide")
    level = lax.axis_index("narrow")
    above = (wide, lax.rem(level + 1, DEPTH))
    below = (wide, lax.rem(level + DEPTH - 1, DEPTH))

    load = pltpu.make_async_copy(features, held, load_sem)
    load.start()
    barrier = pltpu.get_barrier_semaphore()
    for neighbour in (above, below):
        pl.semaphore_signal(barrier, inc=1, device_id=neighbour, device_id_type=MESH)
    pl.semaphore_wait(barrier, 2)

    running = running_counts(occupied)
    halos = functools.partial(halo_copies, tiles, halo_send, halo_recv, above, below)
    edges = functools.partial(
        edge_copies, low, high, from_upper, from_lower, edge_send, edge_recv, above, below
    )
    load.wait()

    @pl.loop(0, slots)
    def _(s):
        tiles[s, :, 16:80, :] = held[block_of_rank(running, s)]
        for copy in halos(s):
            copy.start()

    for planes in (acts_in, acts_mid):
        planes[0:TAPS, :] = jnp.zeros((TAPS, BX), bf16)
        planes[(TZ + 1) * TAPS : (TZ + 2) * TAPS, :] = jnp.zeros((TAPS, BX), bf16)
    build_banded(taps_one, mixed, w_one)
    build_banded(taps_two, mixed, w_two)
    build_head(w_head, w_top)

    work_through(
        slots,
        level,
        tiles,
        acts_in,
        acts_mid,
        w_one,
        w_two,
        w_top,
        result,
        low,
        high,
        finished,
        from_lower,
        from_upper,
        halos,
        edges,
        lambda s: None,
    )

    for b in range(BLK):
        kept = finished[running[b] - occupied[b]]
        out[b] = jnp.where(occupied[b] > 0, kept, jnp.zeros_like(kept))


SLOTS = 7
SURE = 3
GROUPS = ((0, 4, 3), (4, 8, 4), (8, 10, 5))
LANES = 10
TWINS = 4
TARGETS = (6, 5)
COLUMNS = 32


def lane_step(lane, core):
    if lane < 8:
        sign = (1, -1, 1, -1)[lane - TWINS]
        return (sign, 0) if lane < TWINS + 2 else (0, sign)
    sign = (1, -1)[lane - 8]
    return sign * (1 - core), sign * core


def column_at(x, y, core):
    return (x % 4 * 4 + y % 4) * 2 + core


def lane_columns(lane, sign):
    column = lax.axis_index("wide")
    core, y, x = column % 2, column // 2 % 4, column // 8
    if lane < TWINS:
        return column_at(x, y, 1 - core)
    over_x, over_y = lane_step(lane, core)
    return column_at(x + sign * over_x + 4, y + sign * over_y + 4, core)


def turned(value, dim, step):
    step = step % 4
    if step == 0:
        return value
    head = lax.slice_in_dim(value, 0, step, axis=dim)
    return jnp.concatenate([lax.slice_in_dim(value, step, 4, axis=dim), head], axis=dim)


def across(value, kind, sign):
    if kind == 0:
        return jnp.concatenate([value[:, :, 1:2], value[:, :, 0:1]], axis=2)
    if kind < 5:
        over_x, over_y = lane_step(kind + TWINS - 1, 0)
        return turned(turned(value, 0, sign * over_x), 1, sign * over_y)
    step = sign * (1, -1)[kind - 5]
    over_x, over_y = turned(value, 0, step), turned(value, 1, step)
    return jnp.concatenate([over_x[:, :, 0:1], over_y[:, :, 1:2]], axis=2)


def make_plan(counts, used):
    load = counts
    own = counts
    for turn, target in enumerate(TARGETS):
        for kind in (0, 5, 6, 1, 2, 3, 4):
            gap = load - across(load, kind, 1)
            before = used[kind].reshape(load.shape) if turn > 0 else jnp.zeros_like(load)
            if kind == 0:
                sends = jnp.minimum(jnp.minimum(TWINS - before, own), gap >> 1)
                sends = jnp.maximum(jnp.minimum(sends, load - target), 0)
            else:
                sends = (load > target) & (gap >= 2) & (own > 0) & (before == 0)
                sends = jnp.where(sends, 1, 0)
            used[kind] = (before + sends).reshape(used.shape[1:])
            own = own - sends
            load = load - sends + across(sends, kind, -1)
    need = jnp.maximum(own, SURE)
    for kinds, start in (((0,), 3), ((1, 2, 3, 4), 4), ((5, 6), 5)):
        taken = jnp.zeros_like(load)
        for kind in kinds:
            taken = taken + across(used[kind].reshape(load.shape), kind, -1)
        need = jnp.where(taken > 0, jnp.maximum(need, start) + taken, need)
    used[7, 0] = jnp.max(need.reshape((COLUMNS,) + need.shape[3:]), axis=0)


def shared_kernel(
    occupied,
    features,
    taps_one,
    taps_two,
    w_head,
    out,
    needed,
    held,
    tiles,
    acts_in,
    acts_mid,
    w_one,
    w_two,
    w_top,
    mixed,
    result,
    low,
    high,
    from_upper,
    from_lower,
    finished,
    counts,
    used,
    out_a,
    out_b,
    out_c,
    in_a,
    in_b,
    in_c,
    back_out,
    back_in,
    load_sem,
    count_send,
    count_recv,
    lane_send,
    lane_recv,
    back_send,
    back_recv,
    halo_send,
    halo_recv,
    edge_send,
    edge_recv,
):
    wide = lax.axis_index("wide")
    level = lax.axis_index("narrow")
    above = (wide, lax.rem(level + 1, DEPTH))
    below = (wide, lax.rem(level + DEPTH - 1, DEPTH))

    core, y, x = wide % 2, wide // 2 % 4, wide // 8

    load = pltpu.make_async_copy(features, held, load_sem)
    load.start()
    peers = [
        [column_at(x, y, 1 - core)],
        [column_at(x, y + d, core) for d in (1, 2, 3)],
        [column_at(x + d, y, core) for d in (1, 2, 3)],
    ]
    barrier = pltpu.get_barrier_semaphore()
    greeted = [above, below] + [(column, level) for part in peers for column in part]
    for device in greeted:
        pl.semaphore_signal(barrier, inc=1, device_id=device, device_id_type=MESH)

    running = running_counts(occupied)
    held_blocks = running[-1]
    counts[x, y, core] = jnp.full((8, 128), held_blocks, jnp.int32)
    parts = [counts.at[x, y, core], counts.at[x, y], counts.at[x]]

    def count_copies(turn):
        copies = []
        for d, column in enumerate(peers[turn]):
            at = 3 * turn + d
            copies.append(
                pltpu.make_async_remote_copy(
                    src_ref=parts[turn],
                    dst_ref=parts[turn],
                    send_sem=count_send.at[at],
                    recv_sem=count_recv.at[at],
                    device_id=(column, level),
                    device_id_type=MESH,
                )
            )
        return copies

    outs, ins = (out_a, out_b, out_c), (in_a, in_b, in_c)

    def lane_copy(group, lane):
        at = lane - GROUPS[group][0]
        return pltpu.make_async_remote_copy(
            src_ref=outs[group].at[at],
            dst_ref=ins[group].at[at],
            send_sem=lane_send.at[lane],
            recv_sem=lane_recv.at[lane],
            device_id=(lane_columns(lane, 1), level),
            device_id_type=MESH,
        )

    def back_copy(lane):
        return pltpu.make_async_remote_copy(
            src_ref=back_out.at[lane],
            dst_ref=back_in.at[lane],
            send_sem=back_send.at[lane],
            recv_sem=back_recv.at[lane],
            device_id=(lane_columns(lane, -1), level),
            device_id_type=MESH,
        )

    halos = functools.partial(halo_copies, tiles, halo_send, halo_recv, above, below)
    edges = functools.partial(
        edge_copies, low, high, from_upper, from_lower, edge_send, edge_recv, above, below
    )

    pl.semaphore_wait(barrier, len(greeted))
    for copy in count_copies(0):
        copy.start()
    build_banded(taps_one, mixed, w_one)
    for copy in count_copies(0):
        copy.wait()
    for copy in count_copies(1):
        copy.start()
    build_banded(taps_two, mixed, w_two)
    for copy in count_copies(1):
        copy.wait()
    for copy in count_copies(2):
        copy.start()
    load.wait()

    def stage_own(s):
        tiles[s, :, 16:80, :] = held[block_of_rank(running, s)]
        for copy in halos(s):
            copy.start()

    stage_own(0)
    build_head(w_head, w_top)
    for planes in (acts_in, acts_mid):
        planes[0:TAPS, :] = jnp.zeros((TAPS, BX), bf16)
        planes[(TZ + 1) * TAPS : (TZ + 2) * TAPS, :] = jnp.zeros((TAPS, BX), bf16)
    for copy in count_copies(2):
        copy.wait()
    make_plan(counts[...], used)
    needed[0] = used[7, 0, 0, 0]

    def schedule():
        sent, taken = [], []
        for lane in range(LANES):
            source = lane_columns(lane, -1)
            if lane < TWINS:
                sent.append(jnp.where(used[0, wide, 0, 0] > lane, 1, 0))
                taken.append(jnp.where(used[0, source, 0, 0] > lane, 1, 0))
            else:
                sent.append(used[lane - TWINS + 1, wide, 0, 0])
                taken.append(used[lane - TWINS + 1, source, 0, 0])
        kept = held_blocks - sum(sent)
        ranks = []
        rank = kept
        for lane in range(LANES):
            ranks.append(rank)
            rank = rank + sent[lane]
        places = []
        place = jnp.maximum(kept, SURE)
        for start, end, first in GROUPS:
            place = jnp.maximum(place, first)
            for lane in range(start, end):
                places.append(place)
                place = place + taken[lane]
        return kept, sent, ranks, taken, places

    def send(group):
        ranks = schedule()[2]
        start, end, _ = GROUPS[group]
        for lane in range(start, end):
            outs[group][lane - start] = held[block_of_rank(running, ranks[lane])]
            lane_copy(group, lane).start()

    def receive(group):
        for lane in range(*GROUPS[group][:2]):
            lane_copy(group, lane).wait()

    def stage(s):
        _, _, _, taken, places = schedule()
        value = held[block_of_rank(running, s)]
        for group, (start, end, first) in enumerate(GROUPS):
            if s < first:
                continue
            chosen, found = jnp.int32(0), jnp.int32(0)
            for lane in range(start, end):
                here = (taken[lane] > 0) & (places[lane] == s)
                chosen = chosen + jnp.where(here, lane - start, 0)
                found = found + jnp.where(here, 1, 0)
            value = jnp.where(found > 0, ins[group][chosen], value)
        tiles[s, :, 16:80, :] = value
        for copy in halos(s):
            copy.start()

    def before(s):
        @pl.when(s < SURE - 1)
        def _():
            stage_own(s + 1)

        @pl.when(s == 2)
        def _():
            receive(0)
            stage(3)
            send(2)

        @pl.when(s == 3)
        def _():
            receive(1)
            stage(4)

        @pl.when(s == 4)
        def _():
            receive(2)
            stage(5)

        @pl.when(s == 5)
        def _():
            stage(6)

    send(1)
    send(0)
    work_through(
        SLOTS,
        level,
        tiles,
        acts_in,
        acts_mid,
        w_one,
        w_two,
        w_top,
        result,
        low,
        high,
        finished,
        from_lower,
        from_upper,
        halos,
        edges,
        before,
    )

    kept, sent, ranks, _, places = schedule()
    for lane in reversed(range(LANES)):
        back_out[lane] = finished[jnp.clip(places[lane], 0, SLOTS - 1)]
        back_copy(lane).start()
    for lane in range(LANES):
        back_copy(lane).wait()

    for b in range(BLK):
        rank = running[b] - occupied[b]
        chosen = jnp.int32(0)
        for lane in range(LANES):
            chosen = chosen + jnp.where((sent[lane] > 0) & (ranks[lane] == rank), lane, 0)
        local = finished[jnp.minimum(rank, SLOTS - 1)]
        value = jnp.where(rank < kept, local, back_in[chosen])
        out[b] = jnp.where(occupied[b] > 0, value, jnp.zeros_like(value))


def work_scratch(slots):
    return [
        pltpu.VMEM((BLK, C, ZD * BY, BX), bf16),
        pltpu.VMEM((slots, C, TZ * BY, BX), bf16),
        pltpu.VMEM(((TZ + 2) * TAPS, BX), bf16),
        pltpu.VMEM(((TZ + 2) * TAPS, BX), bf16),
        pltpu.VMEM((ROWS, 9 * ROWS), bf16),
        pltpu.VMEM((ROWS, 9 * ROWS), bf16),
        pltpu.VMEM((AFF * BY, ROWS), bf16),
        pltpu.VMEM((ROWS, 9 * ROWS), bf16),
        pltpu.VMEM((slots, ZD, AFF * BY, BX), f32),
        pltpu.VMEM((slots, 2 * AFF * BY, BX), bf16),
        pltpu.VMEM((slots, 2 * AFF * BY, BX), bf16),
        pltpu.VMEM((slots, 2 * AFF * BY, BX), bf16),
        pltpu.VMEM((slots, 2 * AFF * BY, BX), bf16),
        pltpu.VMEM((slots, AFF, ZD * BY, BX), bf16),
    ]


def on_device(features, occupied, w_first, w_second, w_head):
    vmem = pl.BlockSpec(memory_space=pltpu.VMEM)
    in_specs = [
        pl.BlockSpec(memory_space=pltpu.SMEM),
        pl.BlockSpec(memory_space=pl.ANY),
        vmem,
        vmem,
        vmem,
    ]
    affinities = jax.ShapeDtypeStruct((BLK, AFF, ZD * BY, BX), bf16)
    dma = pltpu.SemaphoreType.DMA
    shared = pl.pallas_call(
        shared_kernel,
        out_shape=[affinities, jax.ShapeDtypeStruct((1,), jnp.int32)],
        in_specs=in_specs,
        out_specs=[vmem, pl.BlockSpec(memory_space=pltpu.SMEM)],
        scratch_shapes=work_scratch(SLOTS)
        + [
            pltpu.VMEM((4, 4, 2, 8, 128), jnp.int32),
            pltpu.VMEM((8, COLUMNS, 8, 128), jnp.int32),
        ]
        + [pltpu.VMEM((end - start, C, ZD * BY, BX), bf16) for start, end, _ in GROUPS * 2]
        + [
            pltpu.VMEM((LANES, AFF, ZD * BY, BX), bf16),
            pltpu.VMEM((LANES, AFF, ZD * BY, BX), bf16),
            dma,
            dma((9,)),
            dma((9,)),
            dma((LANES,)),
            dma((LANES,)),
            dma((LANES,)),
            dma((LANES,)),
            dma((SLOTS, 2)),
            dma((SLOTS, 2)),
            dma((SLOTS, 2)),
            dma((SLOTS, 2)),
        ],
        compiler_params=pltpu.CompilerParams(
            collective_id=0, has_side_effects=True, vmem_limit_bytes=56 << 20
        ),
    )
    whole = pl.pallas_call(
        functools.partial(whole_kernel, BLK),
        out_shape=affinities,
        in_specs=in_specs,
        out_specs=vmem,
        scratch_shapes=work_scratch(BLK)
        + [dma, dma((BLK, 2)), dma((BLK, 2)), dma((BLK, 2)), dma((BLK, 2))],
        compiler_params=pltpu.CompilerParams(
            collective_id=1, has_side_effects=True, vmem_limit_bytes=56 << 20
        ),
    )
    taps = [
        jnp.transpose(w, (2, 3, 4, 0, 1)).reshape(27 * C, C) for w in (w_first, w_second)
    ]
    args = (occupied, features.reshape(BLK, C, ZD * BY, BX), *taps, w_head)
    out, needed = shared(*args)
    out = lax.cond(needed[0] > SLOTS, lambda: whole(*args), lambda: out)
    return out.reshape(BLK, AFF, ZD, BY, BX)


def solution(mesh):
    in_specs = (P("wide", None, "narrow", None, None), P("wide"), P(), P(), P())
    out_specs = P("wide", None, "narrow", None, None)
    return jax.shard_map(
        on_device, mesh=mesh, in_specs=in_specs, out_specs=out_specs, check_vma=False
    )
```

```python
import functools

import jax
import jax.numpy as jnp
from jax import lax
from jax.experimental import pallas as pl
from jax.experimental.pallas import tpu as pltpu
from jax.sharding import PartitionSpec as P

C = 32
AFF = 3
BLK = 16
BY = 8
BX = 128
ZD = 8
TZ = 12
ROWS = C * BY
TAPS = 3 * ROWS
BLEND = tuple(min(1.0, (t + 0.5) / 4, (TZ - t - 0.5) / 4) for t in range(TZ))
MESH = pl.DeviceIdType.MESH
f32 = jnp.float32
bf16 = jnp.bfloat16


def iota(shape, dim):
    return lax.broadcasted_iota(jnp.int32, shape, dim)


def put_shifted(planes, z, value, first, last):
    base = (z + 1) * TAPS
    value = value.astype(bf16)
    nothing = jnp.zeros_like(value)
    planes[base : base + ROWS, :] = jnp.where(first, nothing, pltpu.roll(value, 1, 1))
    planes[base + ROWS : base + 2 * ROWS, :] = value
    planes[base + 2 * ROWS : base + TAPS, :] = jnp.where(
        last, nothing, pltpu.roll(value, BX - 1, 1)
    )


def conv_pair(planes, weight, pair):
    base = 2 * pair * TAPS
    gathered = jnp.concatenate(
        [planes[base : base + 3 * TAPS, :], planes[base + TAPS : base + 4 * TAPS, :]], axis=1
    )
    return jnp.dot(weight[...], gathered, preferred_element_type=f32)


def work_through(
    slots,
    level,
    tiles,
    acts_in,
    acts_mid,
    w_one,
    w_two,
    w_top,
    result,
    low,
    high,
    finished,
    from_lower,
    from_upper,
    halos,
    edges,
    before,
):
    lane = iota((ROWS, BX), 1)
    first, last = lane == 0, lane == BX - 1

    def prepare(s, p):
        value = tiles[s, :, 16 * p : 16 * p + 16, :].astype(f32)
        if p == 0:
            value = jnp.where(level > 0, value, 0.0)
        if p == 5:
            value = jnp.where(level < DEPTH - 1, value, 0.0)
        value = value.reshape(C, 2, BY, BX)
        put_shifted(acts_in, 2 * p, value[:, 0].reshape(ROWS, BX), first, last)
        put_shifted(acts_in, 2 * p + 1, value[:, 1].reshape(ROWS, BX), first, last)

    def conv_one(p):
        value = jnp.maximum(conv_pair(acts_in, w_one, p), 0.0)
        put_shifted(acts_mid, 2 * p, value[:, :BX], first, last)
        put_shifted(acts_mid, 2 * p + 1, value[:, BX:], first, last)

    def conv_two(p):
        base = (2 * p + 1) * TAPS + ROWS
        own = jnp.concatenate(
            [acts_in[base : base + ROWS, :], acts_in[base + TAPS : base + TAPS + ROWS, :]], axis=1
        )
        value = conv_pair(acts_mid, w_two, p) + own.astype(f32)
        return jnp.maximum(value, 0.0).astype(bf16)

    def head(s, p, acts):
        value = jnp.dot(w_top[...], acts, preferred_element_type=f32)
        pair = [value[:, :BX] * BLEND[2 * p], value[:, BX:] * BLEND[2 * p + 1]]
        if p == 0:
            low[s] = jnp.concatenate(pair, axis=0).astype(bf16)
        elif p == 5:
            high[s] = jnp.concatenate(pair, axis=0).astype(bf16)
        else:
            result[s, 2 * p - 2] = pair[0]
            result[s, 2 * p - 1] = pair[1]

    def close(s):
        for copy in edges(s):
            copy.wait()
        finish(result, from_lower, from_upper, finished, s, level)

    @pl.loop(0, slots)
    def _(s):
        before(s)

        @pl.when(s > 1)
        def _():
            for copy in edges(s - 2):
                copy.start()

        @pl.when(s > 2)
        def _():
            close(s - 3)

        for copy in halos(s):
            copy.wait()
        previous = jnp.maximum(s - 1, 0)
        acts_4 = conv_two(4)
        prepare(s, 0)
        prepare(s, 1)
        acts_5 = conv_two(5)
        conv_one(0)
        prepare(s, 2)
        head(previous, 4, acts_4)
        conv_one(1)
        prepare(s, 3)
        head(previous, 5, acts_5)
        conv_one(2)
        prepare(s, 4)
        acts_0 = conv_two(0)
        conv_one(3)
        prepare(s, 5)
        acts_1 = conv_two(1)
        head(s, 0, acts_0)
        conv_one(4)
        acts_2 = conv_two(2)
        head(s, 1, acts_1)
        conv_one(5)
        acts_3 = conv_two(3)
        head(s, 2, acts_2)
        head(s, 3, acts_3)

    for copy in edges(slots - 2):
        copy.start()
    acts_4 = conv_two(4)
    acts_5 = conv_two(5)
    head(slots - 1, 4, acts_4)
    head(slots - 1, 5, acts_5)
    for copy in edges(slots - 1):
        copy.start()
    for s in range(slots - 3, slots):
        close(s)


def build_banded(taps, mixed, banded):
    blocks = []
    for outer in range(9):
        rows = [((outer // 3 * 3 + dy) * 3 + outer % 3) * C for dy in range(3)]
        blocks.append(
            jnp.concatenate([taps[at : at + C, :].astype(f32) for at in rows], axis=1)
        )
    stacked = jnp.concatenate(blocks, axis=0).astype(bf16)
    row, col = iota((3 * C, ROWS), 0), iota((3 * C, ROWS), 1)
    same = row % C == col // BY
    for y in range(BY):
        spread = (same & (col % BY == y + row // C - 1)).astype(bf16)
        wide = jnp.dot(stacked, spread, preferred_element_type=f32).astype(bf16)
        for outer in range(9):
            mixed[y * C : (y + 1) * C, outer * ROWS : (outer + 1) * ROWS] = wide[
                outer * C : (outer + 1) * C
            ]
    row, col = iota((ROWS, ROWS), 0), iota((ROWS, ROWS), 1)
    order = ((row // BY == col % C) & (row % BY == col // C)).astype(bf16)
    for outer in range(9):
        cut = slice(outer * ROWS, (outer + 1) * ROWS)
        banded[:, cut] = jnp.dot(order, mixed[:, cut], preferred_element_type=f32).astype(bf16)


def build_head(w_head, banded):
    spread = (iota((C, ROWS), 1) // BY == iota((C, ROWS), 0)).astype(bf16)
    wide = jnp.dot(w_head[...], spread, preferred_element_type=f32)
    wide = jnp.broadcast_to(wide[:, None, :], (AFF, BY, ROWS)).reshape(AFF * BY, ROWS)
    apart = iota((AFF * BY, ROWS), 1) % BY - iota((AFF * BY, ROWS), 0) % BY
    banded[...] = jnp.where(apart == 0, wide, 0.0).astype(bf16)


DEPTH = 4


def running_counts(occupied):
    running = []
    count = jnp.int32(0)
    for b in range(BLK):
        count = count + occupied[b]
        running.append(count)
    return running


def block_of_rank(running, rank):
    picked = jnp.int32(0)
    for b in range(BLK):
        picked = picked + jnp.where(running[b] <= rank, 1, 0)
    return jnp.minimum(picked, BLK - 1)


def halo_copies(tiles, send, recv, above, below, s):
    down = pltpu.make_async_remote_copy(
        src_ref=tiles.at[s, :, 16:32, :],
        dst_ref=tiles.at[s, :, 80:96, :],
        send_sem=send.at[s, 0],
        recv_sem=recv.at[s, 0],
        device_id=below,
        device_id_type=MESH,
    )
    up = pltpu.make_async_remote_copy(
        src_ref=tiles.at[s, :, 64:80, :],
        dst_ref=tiles.at[s, :, 0:16, :],
        send_sem=send.at[s, 1],
        recv_sem=recv.at[s, 1],
        device_id=above,
        device_id_type=MESH,
    )
    return down, up


def edge_copies(low, high, from_upper, from_lower, send, recv, above, below, s):
    down = pltpu.make_async_remote_copy(
        src_ref=low.at[s],
        dst_ref=from_upper.at[s],
        send_sem=send.at[s, 0],
        recv_sem=recv.at[s, 0],
        device_id=below,
        device_id_type=MESH,
    )
    up = pltpu.make_async_remote_copy(
        src_ref=high.at[s],
        dst_ref=from_lower.at[s],
        send_sem=send.at[s, 1],
        recv_sem=recv.at[s, 1],
        device_id=above,
        device_id_type=MESH,
    )
    return down, up


def finish(result, from_lower, from_upper, finished, s, level):
    has_lower, has_upper = level > 0, level < DEPTH - 1
    planes = [result[s, z] for z in range(ZD)]
    lower = from_lower[s].astype(f32)
    upper = from_upper[s].astype(f32)
    for i in range(2):
        part = lower[24 * i : 24 * i + 24]
        planes[i] = jnp.where(has_lower, planes[i] + part, planes[i] / BLEND[2 + i])
        part = upper[24 * i : 24 * i + 24]
        planes[6 + i] = jnp.where(has_upper, planes[6 + i] + part, planes[6 + i] / BLEND[8 + i])
    for a in range(AFF):
        for p in range(4):
            two = [planes[2 * p + i][BY * a : BY * a + BY] for i in range(2)]
            finished[s, a, 16 * p : 16 * p + 16, :] = jnp.concatenate(two, axis=0).astype(bf16)


def whole_kernel(
    slots,
    occupied,
    features,
    taps_one,
    taps_two,
    w_head,
    out,
    held,
    tiles,
    acts_in,
    acts_mid,
    w_one,
    w_two,
    w_top,
    mixed,
    result,
    low,
    high,
    from_upper,
    from_lower,
    finished,
    load_sem,
    halo_send,
    halo_recv,
    edge_send,
    edge_recv,
):
    wide = lax.axis_index("wide")
    level = lax.axis_index("narrow")
    above = (wide, lax.rem(level + 1, DEPTH))
    below = (wide, lax.rem(level + DEPTH - 1, DEPTH))

    load = pltpu.make_async_copy(features, held, load_sem)
    load.start()
    barrier = pltpu.get_barrier_semaphore()
    for neighbour in (above, below):
        pl.semaphore_signal(barrier, inc=1, device_id=neighbour, device_id_type=MESH)
    pl.semaphore_wait(barrier, 2)

    running = running_counts(occupied)
    halos = functools.partial(halo_copies, tiles, halo_send, halo_recv, above, below)
    edges = functools.partial(
        edge_copies, low, high, from_upper, from_lower, edge_send, edge_recv, above, below
    )
    load.wait()

    @pl.loop(0, slots)
    def _(s):
        tiles[s, :, 16:80, :] = held[block_of_rank(running, s)]
        for copy in halos(s):
            copy.start()

    for planes in (acts_in, acts_mid):
        planes[0:TAPS, :] = jnp.zeros((TAPS, BX), bf16)
        planes[(TZ + 1) * TAPS : (TZ + 2) * TAPS, :] = jnp.zeros((TAPS, BX), bf16)
    build_banded(taps_one, mixed, w_one)
    build_banded(taps_two, mixed, w_two)
    build_head(w_head, w_top)

    work_through(
        slots,
        level,
        tiles,
        acts_in,
        acts_mid,
        w_one,
        w_two,
        w_top,
        result,
        low,
        high,
        finished,
        from_lower,
        from_upper,
        halos,
        edges,
        lambda s: None,
    )

    for b in range(BLK):
        kept = finished[running[b] - occupied[b]]
        out[b] = jnp.where(occupied[b] > 0, kept, jnp.zeros_like(kept))


SLOTS = 7
SURE = 2
GROUPS = ((0, 4, 2), (4, 8, 4), (8, 10, 5))
LANES = 10
TWINS = 4
TURNS = (
    (6, (0, 5, 6, 1, 2, 3, 4)),
    (5, (1, 2, 3, 4, 5, 6, 0)),
    (5, (0, 5, 6, 1, 2, 3, 4)),
)
COLUMNS = 32


def lane_step(lane, core):
    if lane < 8:
        sign = (1, -1, 1, -1)[lane - TWINS]
        return (sign, 0) if lane < TWINS + 2 else (0, sign)
    sign = (1, -1)[lane - 8]
    return sign * (1 - core), sign * core


def column_at(x, y, core):
    return (x % 4 * 4 + y % 4) * 2 + core


def lane_columns(lane, sign):
    column = lax.axis_index("wide")
    core, y, x = column % 2, column // 2 % 4, column // 8
    if lane < TWINS:
        return column_at(x, y, 1 - core)
    over_x, over_y = lane_step(lane, core)
    return column_at(x + sign * over_x + 4, y + sign * over_y + 4, core)


def turned(value, dim, step):
    step = step % 4
    if step == 0:
        return value
    head = lax.slice_in_dim(value, 0, step, axis=dim)
    return jnp.concatenate([lax.slice_in_dim(value, step, 4, axis=dim), head], axis=dim)


def across(value, kind, sign):
    if kind == 0:
        return jnp.concatenate([value[:, :, 1:2], value[:, :, 0:1]], axis=2)
    if kind < 5:
        over_x, over_y = lane_step(kind + TWINS - 1, 0)
        return turned(turned(value, 0, sign * over_x), 1, sign * over_y)
    step = sign * (1, -1)[kind - 5]
    over_x, over_y = turned(value, 0, step), turned(value, 1, step)
    return jnp.concatenate([over_x[:, :, 0:1], over_y[:, :, 1:2]], axis=2)


def make_plan(counts, used):
    load = counts
    own = counts
    for turn, (target, order) in enumerate(TURNS):
        for kind in order:
            gap = load - across(load, kind, 1)
            before = used[kind].reshape(load.shape) if turn > 0 else jnp.zeros_like(load)
            if kind == 0:
                sends = jnp.minimum(jnp.minimum(TWINS - before, own), gap >> 1)
                sends = jnp.maximum(jnp.minimum(sends, load - target), 0)
            else:
                sends = (load > target) & (gap >= 2) & (own > 0) & (before == 0)
                sends = jnp.where(sends, 1, 0)
            used[kind] = (before + sends).reshape(used.shape[1:])
            own = own - sends
            load = load - sends + across(sends, kind, -1)
    need = jnp.maximum(own, SURE)
    for kinds, start in (((0,), 2), ((1, 2, 3, 4), 4), ((5, 6), 5)):
        taken = jnp.zeros_like(load)
        for kind in kinds:
            taken = taken + across(used[kind].reshape(load.shape), kind, -1)
        need = jnp.where(taken > 0, jnp.maximum(need, start) + taken, need)
    used[7, 0] = jnp.max(need.reshape((COLUMNS,) + need.shape[3:]), axis=0)


def shared_kernel(
    occupied,
    features,
    taps_one,
    taps_two,
    w_head,
    out,
    needed,
    held,
    tiles,
    acts_in,
    acts_mid,
    w_one,
    w_two,
    w_top,
    mixed,
    result,
    low,
    high,
    from_upper,
    from_lower,
    finished,
    counts,
    used,
    out_a,
    out_b,
    out_c,
    in_a,
    in_b,
    in_c,
    back_out,
    back_in,
    load_sem,
    count_send,
    count_recv,
    lane_send,
    lane_recv,
    back_send,
    back_recv,
    halo_send,
    halo_recv,
    edge_send,
    edge_recv,
):
    wide = lax.axis_index("wide")
    level = lax.axis_index("narrow")
    above = (wide, lax.rem(level + 1, DEPTH))
    below = (wide, lax.rem(level + DEPTH - 1, DEPTH))

    core, y, x = wide % 2, wide // 2 % 4, wide // 8

    load = pltpu.make_async_copy(features, held, load_sem)
    load.start()
    peers = [
        [column_at(x, y, 1 - core)],
        [column_at(x, y + d, core) for d in (1, 2, 3)],
        [column_at(x + d, y, core) for d in (1, 2, 3)],
    ]
    barrier = pltpu.get_barrier_semaphore()
    greeted = [above, below] + [(column, level) for part in peers for column in part]
    for device in greeted:
        pl.semaphore_signal(barrier, inc=1, device_id=device, device_id_type=MESH)

    running = running_counts(occupied)
    held_blocks = running[-1]
    counts[x, y, core] = jnp.full((8, 128), held_blocks, jnp.int32)
    parts = [counts.at[x, y, core], counts.at[x, y], counts.at[x]]

    def count_copies(turn):
        copies = []
        for d, column in enumerate(peers[turn]):
            at = 3 * turn + d
            copies.append(
                pltpu.make_async_remote_copy(
                    src_ref=parts[turn],
                    dst_ref=parts[turn],
                    send_sem=count_send.at[at],
                    recv_sem=count_recv.at[at],
                    device_id=(column, level),
                    device_id_type=MESH,
                )
            )
        return copies

    outs, ins = (out_a, out_b, out_c), (in_a, in_b, in_c)

    def lane_copy(group, lane):
        at = lane - GROUPS[group][0]
        return pltpu.make_async_remote_copy(
            src_ref=outs[group].at[at],
            dst_ref=ins[group].at[at],
            send_sem=lane_send.at[lane],
            recv_sem=lane_recv.at[lane],
            device_id=(lane_columns(lane, 1), level),
            device_id_type=MESH,
        )

    def back_copy(lane):
        return pltpu.make_async_remote_copy(
            src_ref=back_out.at[lane],
            dst_ref=back_in.at[lane],
            send_sem=back_send.at[lane],
            recv_sem=back_recv.at[lane],
            device_id=(lane_columns(lane, -1), level),
            device_id_type=MESH,
        )

    halos = functools.partial(halo_copies, tiles, halo_send, halo_recv, above, below)
    edges = functools.partial(
        edge_copies, low, high, from_upper, from_lower, edge_send, edge_recv, above, below
    )

    pl.semaphore_wait(barrier, len(greeted))
    for copy in count_copies(0):
        copy.start()
    build_banded(taps_one, mixed, w_one)
    for copy in count_copies(0):
        copy.wait()
    for copy in count_copies(1):
        copy.start()
    build_banded(taps_two, mixed, w_two)
    for copy in count_copies(1):
        copy.wait()
    for copy in count_copies(2):
        copy.start()
    load.wait()

    def stage_own(s):
        tiles[s, :, 16:80, :] = held[block_of_rank(running, s)]
        for copy in halos(s):
            copy.start()

    stage_own(0)
    build_head(w_head, w_top)
    for planes in (acts_in, acts_mid):
        planes[0:TAPS, :] = jnp.zeros((TAPS, BX), bf16)
        planes[(TZ + 1) * TAPS : (TZ + 2) * TAPS, :] = jnp.zeros((TAPS, BX), bf16)
    for copy in count_copies(2):
        copy.wait()
    make_plan(counts[...], used)
    needed[0] = used[7, 0, 0, 0]

    def schedule():
        sent, taken = [], []
        for lane in range(LANES):
            source = lane_columns(lane, -1)
            if lane < TWINS:
                sent.append(jnp.where(used[0, wide, 0, 0] > lane, 1, 0))
                taken.append(jnp.where(used[0, source, 0, 0] > lane, 1, 0))
            else:
                sent.append(used[lane - TWINS + 1, wide, 0, 0])
                taken.append(used[lane - TWINS + 1, source, 0, 0])
        kept = held_blocks - sum(sent)
        ranks = []
        rank = kept
        for lane in range(LANES):
            ranks.append(rank)
            rank = rank + sent[lane]
        places = []
        place = jnp.maximum(kept, SURE)
        for start, end, first in GROUPS:
            place = jnp.maximum(place, first)
            for lane in range(start, end):
                places.append(place)
                place = place + taken[lane]
        return kept, sent, ranks, taken, places

    def send(group):
        ranks = schedule()[2]
        start, end, _ = GROUPS[group]
        for lane in range(start, end):
            outs[group][lane - start] = held[block_of_rank(running, ranks[lane])]
            lane_copy(group, lane).start()

    def receive(group):
        for lane in range(*GROUPS[group][:2]):
            lane_copy(group, lane).wait()

    def stage(s):
        _, _, _, taken, places = schedule()
        value = held[block_of_rank(running, s)]
        for group, (start, end, first) in enumerate(GROUPS):
            if s < first:
                continue
            chosen, found = jnp.int32(0), jnp.int32(0)
            for lane in range(start, end):
                here = (taken[lane] > 0) & (places[lane] == s)
                chosen = chosen + jnp.where(here, lane - start, 0)
                found = found + jnp.where(here, 1, 0)
            value = jnp.where(found > 0, ins[group][chosen], value)
        tiles[s, :, 16:80, :] = value
        for copy in halos(s):
            copy.start()

    def before(s):
        @pl.when(s < SURE - 1)
        def _():
            stage_own(s + 1)

        @pl.when(s == 1)
        def _():
            receive(0)
            stage(2)

        @pl.when(s == 2)
        def _():
            stage(3)
            send(2)

        @pl.when(s == 3)
        def _():
            receive(1)
            stage(4)

        @pl.when(s == 4)
        def _():
            receive(2)
            stage(5)

        @pl.when(s == 5)
        def _():
            stage(6)

    send(1)
    send(0)
    work_through(
        SLOTS,
        level,
        tiles,
        acts_in,
        acts_mid,
        w_one,
        w_two,
        w_top,
        result,
        low,
        high,
        finished,
        from_lower,
        from_upper,
        halos,
        edges,
        before,
    )

    kept, sent, ranks, _, places = schedule()
    for lane in reversed(range(LANES)):
        back_out[lane] = finished[jnp.clip(places[lane], 0, SLOTS - 1)]
        back_copy(lane).start()
    for lane in range(LANES):
        back_copy(lane).wait()

    for b in range(BLK):
        rank = running[b] - occupied[b]
        chosen = jnp.int32(0)
        for lane in range(LANES):
            chosen = chosen + jnp.where((sent[lane] > 0) & (ranks[lane] == rank), lane, 0)
        local = finished[jnp.minimum(rank, SLOTS - 1)]
        value = jnp.where(rank < kept, local, back_in[chosen])
        out[b] = jnp.where(occupied[b] > 0, value, jnp.zeros_like(value))


def work_scratch(slots):
    return [
        pltpu.VMEM((BLK, C, ZD * BY, BX), bf16),
        pltpu.VMEM((slots, C, TZ * BY, BX), bf16),
        pltpu.VMEM(((TZ + 2) * TAPS, BX), bf16),
        pltpu.VMEM(((TZ + 2) * TAPS, BX), bf16),
        pltpu.VMEM((ROWS, 9 * ROWS), bf16),
        pltpu.VMEM((ROWS, 9 * ROWS), bf16),
        pltpu.VMEM((AFF * BY, ROWS), bf16),
        pltpu.VMEM((ROWS, 9 * ROWS), bf16),
        pltpu.VMEM((slots, ZD, AFF * BY, BX), f32),
        pltpu.VMEM((slots, 2 * AFF * BY, BX), bf16),
        pltpu.VMEM((slots, 2 * AFF * BY, BX), bf16),
        pltpu.VMEM((slots, 2 * AFF * BY, BX), bf16),
        pltpu.VMEM((slots, 2 * AFF * BY, BX), bf16),
        pltpu.VMEM((slots, AFF, ZD * BY, BX), bf16),
    ]


def on_device(features, occupied, w_first, w_second, w_head):
    vmem = pl.BlockSpec(memory_space=pltpu.VMEM)
    in_specs = [
        pl.BlockSpec(memory_space=pltpu.SMEM),
        pl.BlockSpec(memory_space=pl.ANY),
        vmem,
        vmem,
        vmem,
    ]
    affinities = jax.ShapeDtypeStruct((BLK, AFF, ZD * BY, BX), bf16)
    dma = pltpu.SemaphoreType.DMA
    shared = pl.pallas_call(
        shared_kernel,
        out_shape=[affinities, jax.ShapeDtypeStruct((1,), jnp.int32)],
        in_specs=in_specs,
        out_specs=[vmem, pl.BlockSpec(memory_space=pltpu.SMEM)],
        scratch_shapes=work_scratch(SLOTS)
        + [
            pltpu.VMEM((4, 4, 2, 8, 128), jnp.int32),
            pltpu.VMEM((8, COLUMNS, 8, 128), jnp.int32),
        ]
        + [pltpu.VMEM((end - start, C, ZD * BY, BX), bf16) for start, end, _ in GROUPS * 2]
        + [
            pltpu.VMEM((LANES, AFF, ZD * BY, BX), bf16),
            pltpu.VMEM((LANES, AFF, ZD * BY, BX), bf16),
            dma,
            dma((9,)),
            dma((9,)),
            dma((LANES,)),
            dma((LANES,)),
            dma((LANES,)),
            dma((LANES,)),
            dma((SLOTS, 2)),
            dma((SLOTS, 2)),
            dma((SLOTS, 2)),
            dma((SLOTS, 2)),
        ],
        compiler_params=pltpu.CompilerParams(
            collective_id=0, has_side_effects=True, vmem_limit_bytes=56 << 20
        ),
    )
    whole = pl.pallas_call(
        functools.partial(whole_kernel, BLK),
        out_shape=affinities,
        in_specs=in_specs,
        out_specs=vmem,
        scratch_shapes=work_scratch(BLK)
        + [dma, dma((BLK, 2)), dma((BLK, 2)), dma((BLK, 2)), dma((BLK, 2))],
        compiler_params=pltpu.CompilerParams(
            collective_id=1, has_side_effects=True, vmem_limit_bytes=56 << 20
        ),
    )
    taps = [
        jnp.transpose(w, (2, 3, 4, 0, 1)).reshape(27 * C, C) for w in (w_first, w_second)
    ]
    args = (occupied, features.reshape(BLK, C, ZD * BY, BX), *taps, w_head)
    out, needed = shared(*args)
    out = lax.cond(needed[0] > SLOTS, lambda: whole(*args), lambda: out)
    return out.reshape(BLK, AFF, ZD, BY, BX)


def solution(mesh):
    in_specs = (P("wide", None, "narrow", None, None), P("wide"), P(), P(), P())
    out_specs = P("wide", None, "narrow", None, None)
    return jax.shard_map(
        on_device, mesh=mesh, in_specs=in_specs, out_specs=out_specs, check_vma=False
    )
```
